512 devices in a mesh: blk: 64 (over z, x_lo, core), grp: 8 (over y, x_hi).
Axes of the slice: x: 4 (x_hi: 2, x_lo: 2; x = x_hi * 2 + x_lo), y: 4, z: 16, core: 2. Of those that a mesh axis runs over, the one named last changes fastest.
Arguments:
- view_one: float32 [131072, 256], P(('blk', 'grp')), may hold values from -4 to 4
- view_two: float32 [131072, 256], P(('blk', 'grp')), may hold values from -4 to 4
- node_ids: int32 [131072], P(('blk', 'grp')), may hold values from 0 to 2999999
Outputs:
- grad_one: float32 [131072, 256], P(('blk', 'grp'))
- grad_two: float32 [131072, 256], P(('blk', 'grp'))
The draws below stay inside these ranges and needn't reach their ends.
Inputs may be any that keep to these rules, and one draw needn't show every extreme that they name: `node_ids`: some ids repeat within the batch.
All inputs are finite; a program needn't handle non-finite values.
Results may differ from the reference program's by a relative error of at most 0.0003.
Values sent between devices are 32-bit elements; how exact they have to be, the bound alone decides.
A program may use at most 64 MiB of HBM per device.

```python
import math
import jax
import jax.numpy as jnp
import numpy as np
from jax import lax

LATENT_DIM_SIZE = 256
ROWS = 256
ROUNDS = 5
NODES = 131072
N_BLK = 64
N_GRP = 8


def cluster_base(key):
    centre_key, member_key, noise_key = jax.random.split(key, 3)
    centres = jax.random.normal(centre_key, (128, LATENT_DIM_SIZE), jnp.float32) * LATENT_DIM_SIZE ** (-0.5)
    member = jax.random.randint(member_key, (NODES,), 0, 128)
    jitter = jax.random.normal(noise_key, (NODES, LATENT_DIM_SIZE), jnp.float32) * (0.8 * LATENT_DIM_SIZE ** (-0.5))
    return jnp.take(centres, member, axis=0) + jitter


def row_scales(key, low, high):
    return jnp.exp(jax.random.uniform(key, (NODES, 1), jnp.float32, math.log(low), math.log(high)))


def draw_view_one(key, part):
    shared_rows = cluster_base(key)
    key = jax.random.fold_in(key, 1)
    row_scale = row_scales(key, 0.5, 2.0)
    return jnp.clip(shared_rows * row_scale, -4.0, 4.0).astype(jnp.float32)


def draw_view_two(key, part):
    shared_rows = cluster_base(key)
    key = jax.random.fold_in(key, 2)
    noise_key, scale_key = jax.random.split(key)
    jitter = jax.random.normal(noise_key, (NODES, LATENT_DIM_SIZE), jnp.float32) * (0.6 * LATENT_DIM_SIZE ** (-0.5))
    row_scale = row_scales(scale_key, 0.5, 2.0)
    return jnp.clip((shared_rows + jitter) * row_scale, -4.0, 4.0).astype(jnp.float32)


def with_ends(values, key, low, high):
    longest = values.shape.index(max(values.shape))
    spots = []
    for shift in (0, 1):
        where = [jax.random.randint(jax.random.fold_in(key, axis), (), 0, length) for axis, length in enumerate(values.shape)]
        where[longest] = (where[longest] + shift) % values.shape[longest]
        spots.append(tuple(where))
    return values.at[spots[0]].set(low).at[spots[1]].set(high)


def ranked_wide(rng, dims, count, skew):
    loads = [min(1 << octave, count + 1 - (1 << octave)) * (1 << 20) // math.isqrt((1 << octave) ** skew) + 1 for octave in range((count + 1).bit_length()) if 1 << octave <= count]
    deviation = 1 + sum(loads) // (1 << 30)
    grid = np.cumsum(np.array([max(1, weight // deviation) for weight in loads]))
    lot = jax.random.randint(jax.random.fold_in(rng, 1), dims, 0, int(grid[len(loads) - 1]))
    start = jnp.left_shift(1, jnp.searchsorted(jnp.asarray(grid, jnp.int32), lot, side="right").astype(jnp.int32))
    grade = start - 1 + jax.random.randint(jax.random.fold_in(rng, 4), dims, 0, 1 << 30) % jnp.minimum(start, count + 1 - start)
    return jax.random.permutation(jax.random.fold_in(rng, 2), count)[grade].astype(jnp.int32)


def setup_inputs(seed: int = 0) -> dict:
    key_of = jax.random.split(jax.random.key(seed), 4)
    return {
        "view_one": draw_view_one(jax.random.fold_in(key_of[3], 71), 0),
        "view_two": draw_view_two(jax.random.fold_in(key_of[3], 71), 0),
        "node_ids": with_ends(ranked_wide(key_of[2], (NODES,), 3000000, 2), jax.random.fold_in(key_of[2], 3), 0, 2999999).astype(jnp.int32),
    }


logit_sharpness_divisor = 0.5

def unit_rows(z):
    radius = jnp.sqrt(lax.optimization_barrier(jnp.sum(z * z, axis=1, keepdims=True)) + 1e-06)
    return (z / radius, radius)

def scored(a, b):
    return jnp.dot(a, b.T, precision=lax.Precision.HIGHEST, preferred_element_type=jnp.float32)

def applied(a, b):
    return jnp.dot(a, b, precision=lax.Precision.HIGHEST, preferred_element_type=jnp.float32)

def window_index(block):
    blocks = [block] + [jnp.bitwise_xor(block, jnp.int32(1 << t)) for t in range(ROUNDS)]
    blocks = jnp.stack(blocks).astype(jnp.int32)
    rows = blocks[:, None] * ROWS + jnp.arange(ROWS, dtype=jnp.int32)[None, :]
    return rows.reshape(-1).astype(jnp.int32)

def masks(block, cols, node_ids):
    own = block * ROWS + jnp.arange(ROWS, dtype=jnp.int32)
    same = node_ids[own][:, None] != node_ids[cols][None, :]
    cross = same | (own[:, None] == cols[None, :])
    return (own, same, cross)

def exps(cosine_logit_matrix, retained_pair_filter):
    return jnp.where(retained_pair_filter, jnp.exp(cosine_logit_matrix / logit_sharpness_divisor), 0.0)

def reference(view_one, view_two, node_ids):
    anchor_node_vectors, radius_one = unit_rows(view_one)
    partnered_node_vectors, radius_two = unit_rows(view_two)
    blocks = jnp.arange(N_BLK * N_GRP, dtype=jnp.int32)

    def first(block):
        cols = window_index(block)
        own, same, cross = masks(block, cols, node_ids)
        ub, vb, uw, vw = (anchor_node_vectors[own], partnered_node_vectors[own], anchor_node_vectors[cols], partnered_node_vectors[cols])
        den_u = lax.optimization_barrier(jnp.sum(exps(scored(ub, vw), cross), axis=1)) + lax.optimization_barrier(jnp.sum(exps(scored(ub, uw), same), axis=1))
        den_v = lax.optimization_barrier(jnp.sum(exps(scored(vb, uw), cross), axis=1)) + lax.optimization_barrier(jnp.sum(exps(scored(vb, vw), same), axis=1))
        return (den_u, den_v)
    den_u, den_v = lax.map(first, blocks)
    inv_u = (1.0 / den_u).reshape(-1)
    inv_v = (1.0 / den_v).reshape(-1)

    def second(block):
        cols = window_index(block)
        own, same, cross = masks(block, cols, node_ids)
        ub, vb, uw, vw = (anchor_node_vectors[own], partnered_node_vectors[own], anchor_node_vectors[cols], partnered_node_vectors[cols])
        iu, iv, iuw, ivw = (inv_u[own], inv_v[own], inv_u[cols], inv_v[cols])
        anchor_node_derivative = applied(exps(scored(ub, vw), cross) * (iu[:, None] + ivw[None, :]), vw)
        anchor_node_derivative = anchor_node_derivative + applied(exps(scored(ub, uw), same) * (iu[:, None] + iuw[None, :]), uw)
        partnered_node_derivative = applied(exps(scored(vb, uw), cross) * (iv[:, None] + iuw[None, :]), uw)
        partnered_node_derivative = partnered_node_derivative + applied(exps(scored(vb, vw), same) * (iv[:, None] + ivw[None, :]), vw)
        return (anchor_node_derivative, partnered_node_derivative)
    anchor_node_derivative, partnered_node_derivative = lax.map(second, blocks)
    anchor_node_derivative = anchor_node_derivative.reshape(-1, LATENT_DIM_SIZE) / (2.0 * logit_sharpness_divisor) - partnered_node_vectors / logit_sharpness_divisor
    partnered_node_derivative = partnered_node_derivative.reshape(-1, LATENT_DIM_SIZE) / (2.0 * logit_sharpness_divisor) - anchor_node_vectors / logit_sharpness_divisor
    grad_one = anchor_node_derivative / radius_one - view_one * lax.optimization_barrier(jnp.sum(view_one * anchor_node_derivative, axis=1, keepdims=True)) / radius_one ** 3
    grad_two = partnered_node_derivative / radius_two - view_two * lax.optimization_barrier(jnp.sum(view_two * partnered_node_derivative, axis=1, keepdims=True)) / radius_two ** 3
    return (grad_one, grad_two)
```

```python
import math

import jax
import jax.numpy as jnp
from jax import lax
from jax.experimental import pallas as pl
from jax.experimental.pallas import tpu as pltpu
from jax.sharding import PartitionSpec as P

MESH = pl.DeviceIdType.MESH
F32, BF16 = jnp.float32, jnp.bfloat16

R = 256
D = 256
CHUNKS = 8
CR = 2 * R // CHUNKS
TAU = 0.5
LOGIT = 1.0 / (TAU * math.log(2.0))
WINDOW = 2
STEPS = 12


def flip(n, bit):
    return n + bit - 2 * bit * ((n // bit) % 2)


def split(x):
    hi = x.astype(BF16)
    return hi, (x - hi.astype(F32)).astype(BF16)


def dot_t(a, b):
    return lax.dot_general(a, b, (((1,), (1,)), ((), ())), preferred_element_type=F32)


def dot(a, b):
    return lax.dot_general(a, b, (((1,), (0,)), ((), ())), preferred_element_type=F32)


def kernel(
    one_hbm, two_hbm, ids_hbm, z, grad, inv_r,
    raw, zl_hi, zl_lo, core_z, streams, k_hi, k_lo, e_hi, e_lo, acc, den_acc, id_col, ids_int, ids, r_ids, id_rows,
    inv_row, r_inv, inv_rows, diag,
    load_sem, direct_send, direct_recv, fwd_send, fwd_recv, core_send, core_recv, ids_send, ids_recv, den_send, den_recv,
):
    blk, grp = lax.axis_index("blk"), lax.axis_index("grp")
    x1 = (flip(blk, 2), grp)
    x3 = (flip(blk, 2), flip(grp, 1))
    y1 = (blk, flip(grp, 2))
    y3 = (blk, flip(flip(grp, 2), 4))
    core = (flip(blk, 1), grp)
    x2 = (blk, flip(grp, 1))
    y2 = (blk, flip(grp, 4))
    partners = (x1, y1, x2, y2, core)

    barrier = pltpu.get_barrier_semaphore()
    for peer in (x1, x3, y1, y3, core, x2, y2):
        pl.semaphore_signal(barrier, inc=1, device_id=peer, device_id_type=MESH)

    loads = [
        pltpu.make_async_copy(one_hbm, raw.at[pl.ds(0, R)], load_sem.at[0]),
        pltpu.make_async_copy(two_hbm, raw.at[pl.ds(R, R)], load_sem.at[1]),
        pltpu.make_async_copy(ids_hbm, ids_int, load_sem.at[2]),
    ]
    for copy in loads:
        copy.start()

    def direct(axis, c):
        return pltpu.make_async_remote_copy(
            src_ref=z.at[pl.ds(CR * c, CR)],
            dst_ref=streams.at[c, axis],
            send_sem=direct_send.at[axis, c],
            recv_sem=direct_recv.at[axis, c],
            device_id=(x1, y1)[axis],
            device_id_type=MESH,
        )

    def forward(axis, c):
        return pltpu.make_async_remote_copy(
            src_ref=streams.at[c, axis],
            dst_ref=streams.at[c, 2 + axis],
            send_sem=fwd_send.at[axis, c],
            recv_sem=fwd_recv.at[axis, c],
            device_id=(x3, y3)[axis],
            device_id_type=MESH,
        )

    to_core = pltpu.make_async_remote_copy(
        src_ref=z, dst_ref=core_z, send_sem=core_send, recv_sem=core_recv, device_id=core, device_id_type=MESH
    )

    def send_ids(p):
        return pltpu.make_async_remote_copy(
            src_ref=ids, dst_ref=r_ids.at[p], send_sem=ids_send.at[p], recv_sem=ids_recv.at[p],
            device_id=partners[p], device_id_type=MESH,
        )

    def send_inv(p):
        return pltpu.make_async_remote_copy(
            src_ref=inv_row, dst_ref=r_inv.at[p], send_sem=den_send.at[p], recv_sem=den_recv.at[p],
            device_id=partners[p], device_id_type=MESH,
        )

    def normalise(c):
        rows = pl.ds(CR * c, CR)
        x = raw[rows]
        ir = lax.rsqrt(jnp.sum(x * x, axis=1, keepdims=True) + 1e-06)
        inv_r[rows] = ir
        z[rows] = x * ir

    loads[0].wait()
    for c in range(CHUNKS):
        if c == CHUNKS // 2:
            loads[1].wait()
        normalise(c)
        if c == 0:
            pl.semaphore_wait(barrier, 7)
        if c < WINDOW:
            direct(0, c).start()
            direct(1, c).start()
    loads[2].wait()
    for q in range(4):
        ids[pl.ds(2 * q, 2)] = ids_int[...].astype(F32)
    for p in range(5):
        send_ids(p).start()
    to_core.start()

    hi, lo = split(z[...] * LOGIT)
    zl_hi[...] = hi
    zl_lo[...] = lo
    d = jnp.exp2(LOGIT * jnp.sum(z[pl.ds(0, R)] * z[pl.ds(R, R)], axis=1, keepdims=True))
    diag[...] = d
    lane = lax.broadcasted_iota(jnp.int32, (R, 128), 1)
    start = jnp.where(lane == 0, d, 0.0)
    den_acc[pl.ds(0, R)] = start
    den_acc[pl.ds(R, R)] = start
    acc[...] = jnp.zeros_like(acc)
    for q in range(2):
        id_col[pl.ds(128 * q, 128)] = jnp.broadcast_to(ids[pl.ds(q, 1)], (128, 128)).T

    def scores(slot, keys, key_ids):
        hi, lo = split(keys)
        k_hi[slot] = hi
        k_lo[...] = lo
        keep = jnp.concatenate([id_col[...], id_col[...]], axis=1) != key_ids
        for h in range(2):
            rows = pl.ds(R * h, R)
            s = dot_t(zl_hi[rows], hi) + dot_t(zl_hi[rows], lo) + dot_t(zl_lo[rows], hi)
            e = jnp.where(keep, jnp.exp2(s), 0.0)
            den_acc[rows] += e[:, :128] + e[:, 128:]
            ehi, elo = split(e)
            e_hi[slot, rows] = ehi
            e_lo[rows] = elo

    def gather(slot):
        for h in range(2):
            rows = pl.ds(R * h, R)
            ehi = e_hi[slot, rows]
            acc[rows] += dot(ehi, k_hi[slot]) + dot(ehi, k_lo[...]) + dot(e_lo[rows], k_hi[slot])

    def pair_ids(ref):
        return jnp.concatenate([ref[pl.ds(0, 1)], ref[pl.ds(1, 1)]], axis=1)

    own_ids = pair_ids(ids)
    for h in range(2):
        scores(h, z[pl.ds(R * h, R)], own_ids)
        gather(h)

    def pass_on(c):
        for axis in range(2):
            direct(axis, c).wait_recv()
            forward(axis, c).start()

        def refill():
            for axis in range(2):
                direct(axis, c).wait_send()
                direct(axis, c + WINDOW).start()

        if isinstance(c, int):
            refill()
        else:
            pl.when(c + WINDOW < CHUNKS)(refill)

    for p in range(5):
        send_ids(p).wait_recv()
    to_core.wait_recv()
    pass_on(0)
    core_ids = pair_ids(r_ids.at[4])
    for h in range(2):
        scores(2 + h, core_z[pl.ds(R * h, R)], core_ids)
        gather(2 + h)
        if h == 0:
            pass_on(1)

    left = lax.broadcasted_iota(jnp.int32, (8, 128), 1) < 64

    def mixed(refs):
        a, b, c, d = (refs[p] for p in range(4))
        turn = lambda x: pltpu.roll(x, 64, 1)
        first = jnp.concatenate([jnp.where(left, a, turn(b)), jnp.where(left, c, turn(d))], axis=1)
        second = jnp.concatenate([jnp.where(left, turn(a), b), jnp.where(left, turn(c), d)], axis=1)
        return first, second

    first, second = mixed(r_ids)
    for q in range(2):
        id_rows[pl.ds(2 * q, 1)] = first[q : q + 1]
        id_rows[pl.ds(2 * q + 1, 1)] = second[q : q + 1]

    def arrived(c):
        for axis in range(2):
            forward(axis, c).wait_recv()

    def stream_scores(c):
        scores(4 + c, streams[c].reshape(4 * CR, D), id_rows[pl.ds(c % 4, 1)])

    def stream_step(c, carry):
        pass_on(c + 2)
        arrived(c)
        stream_scores(c)
        gather(4 + c)
        return carry

    lax.fori_loop(0, CHUNKS - 2, stream_step, 0)
    arrived(CHUNKS - 2)
    stream_scores(CHUNKS - 2)
    gather(4 + CHUNKS - 2)
    arrived(CHUNKS - 1)
    stream_scores(CHUNKS - 1)

    s_hi = den_acc[...].astype(BF16)
    rest = den_acc[...] - s_hi.astype(F32)
    s_mid, s_lo = split(rest)
    ones = jnp.ones((8, 128), BF16)
    sums = dot_t(ones, s_hi) + dot_t(ones, s_mid) + dot_t(ones, s_lo)
    own_inv = 1.0 / sums
    for q in range(4):
        inv_row[pl.ds(q, 1)] = own_inv[0:1, 128 * q : 128 * (q + 1)]
    for q in range(4):
        inv_row[pl.ds(4 + q, 1)] = own_inv[0:1, 128 * q : 128 * (q + 1)]
    for p in range(5):
        send_inv(p).start()

    gather(4 + CHUNKS - 1)
    centre = jnp.mean(own_inv[0:1], axis=1, keepdims=True)
    inv_col = 1.0 / jnp.sum(den_acc[...], axis=1, keepdims=True)
    coef = diag[...] * (inv_col[:R] + inv_col[R:]) - 1.0 / TAU
    for h in range(2):
        rows, others = pl.ds(R * h, R), pl.ds(R * (1 - h), R)
        acc[rows] = (inv_col[R * h : R * (h + 1)] + centre) * acc[rows] + coef * z[others]

    for p in range(5):
        send_inv(p).wait_recv()
    first, second = mixed(r_inv)
    for h in range(2):
        for q in range(2):
            lanes = pl.ds(128 * q, 128)
            inv_rows[pl.ds(h, 1), lanes] = inv_row[pl.ds(2 * h + q, 1)]
            inv_rows[pl.ds(2 + h, 1), lanes] = r_inv[4, pl.ds(2 * h + q, 1)]
    for q in range(4):
        inv_rows[pl.ds(4 + 2 * q, 1)] = first[q : q + 1]
        inv_rows[pl.ds(5 + 2 * q, 1)] = second[q : q + 1]

    for h in range(2):
        rows = pl.ds(R * h, R)
        g = acc[rows]
        for slot in range(STEPS):
            weight = (inv_rows[pl.ds(slot, 1)] - centre).astype(BF16)
            g = g + dot(e_hi[slot, rows] * weight, k_hi[slot])
        grad[rows] = g

    for c in range(CHUNKS):
        for axis in range(2):
            if c >= CHUNKS - WINDOW:
                direct(axis, c).wait_send()
            forward(axis, c).wait_send()
    to_core.wait_send()
    for p in range(5):
        send_ids(p).wait_send()
        send_inv(p).wait_send()


def finish(z, grad, inv_r, out_one, out_two, result, out_sem):
    outs = []
    for c in range(4):
        rows = pl.ds(128 * c, 128)
        g, own = grad[rows], z[rows]
        result[rows] = (g - own * jnp.sum(own * g, axis=1, keepdims=True)) * inv_r[rows]
        copy = pltpu.make_async_copy(
            result.at[rows], (out_one, out_two)[c // 2].at[pl.ds(128 * (c % 2), 128)], out_sem.at[c]
        )
        copy.start()
        outs.append(copy)
    for copy in outs:
        copy.wait()


def on_device(view_one, view_two, node_ids):
    dma = pltpu.SemaphoreType.DMA
    hbm = pl.BlockSpec(memory_space=pltpu.HBM)
    vmem = pl.BlockSpec(memory_space=pltpu.VMEM)
    middle = pl.pallas_call(
        kernel,
        out_shape=(
            pltpu.VMEM((2 * R, D), F32),
            pltpu.VMEM((2 * R, D), F32),
            pltpu.VMEM((2 * R, 1), F32),
        ),
        in_specs=[hbm] * 3,
        out_specs=(vmem,) * 3,
        scratch_shapes=[
            pltpu.VMEM((2 * R, D), F32),
            pltpu.VMEM((2 * R, D), BF16),
            pltpu.VMEM((2 * R, D), BF16),
            pltpu.VMEM((2 * R, D), F32),
            pltpu.VMEM((CHUNKS, 4, CR, D), F32),
            pltpu.VMEM((STEPS, 256, D), BF16),
            pltpu.VMEM((256, D), BF16),
            pltpu.VMEM((STEPS, 2 * R, 256), BF16),
            pltpu.VMEM((2 * R, 256), BF16),
            pltpu.VMEM((2 * R, D), F32),
            pltpu.VMEM((2 * R, 128), F32),
            pltpu.VMEM((R, 128), F32),
            pltpu.VMEM((2, 128), jnp.int32),
            pltpu.VMEM((8, 128), F32),
            pltpu.VMEM((5, 8, 128), F32),
            pltpu.VMEM((8, 256), F32),
            pltpu.VMEM((8, 128), F32),
            pltpu.VMEM((5, 8, 128), F32),
            pltpu.VMEM((16, 256), F32),
            pltpu.VMEM((R, 1), F32),
            dma((3,)),
            dma((2, CHUNKS)),
            dma((2, CHUNKS)),
            dma((2, CHUNKS)),
            dma((2, CHUNKS)),
            dma,
            dma,
            dma((5,)),
            dma((5,)),
            dma((5,)),
            dma((5,)),
        ],
        compiler_params=pltpu.CompilerParams(
            collective_id=0, has_side_effects=True, vmem_limit_bytes=48 * 1024 * 1024
        ),
    )(*(pltpu.with_memory_space_constraint(x, pltpu.HBM) for x in (view_one, view_two, node_ids.reshape(2, 128))))
    return pl.pallas_call(
        finish,
        out_shape=(jax.ShapeDtypeStruct((R, D), F32), jax.ShapeDtypeStruct((R, D), F32)),
        in_specs=[vmem] * 3,
        out_specs=(hbm, hbm),
        scratch_shapes=[pltpu.VMEM((2 * R, D), F32), dma((4,))],
    )(*middle)


def solution(mesh):
    rows = P(("blk", "grp"), None)
    return jax.shard_map(
        on_device,
        mesh=mesh,
        in_specs=(rows, rows, P(("blk", "grp"))),
        out_specs=(rows, rows),
        check_vma=False,
    )
```

```python
import math

import jax
import jax.numpy as jnp
from jax import lax
from jax.experimental import pallas as pl
from jax.experimental.pallas import tpu as pltpu
from jax.sharding import PartitionSpec as P

MESH = pl.DeviceIdType.MESH
F32, BF16 = jnp.float32, jnp.bfloat16

R = 256
D = 256
CHUNKS = 16
CR = 2 * R // CHUNKS
PAIRS = CHUNKS // 2
TAU = 0.5
LOGIT = 1.0 / (TAU * math.log(2.0))
WINDOW = 6
STEPS = 12


def flip(n, bit):
    return n + bit - 2 * bit * ((n // bit) % 2)


def split(x):
    hi = x.astype(BF16)
    return hi, (x - hi.astype(F32)).astype(BF16)


def dot_t(a, b):
    return lax.dot_general(a, b, (((1,), (1,)), ((), ())), preferred_element_type=F32)


def dot(a, b):
    return lax.dot_general(a, b, (((1,), (0,)), ((), ())), preferred_element_type=F32)


def kernel(
    one_hbm, two_hbm, ids_hbm, z, grad, inv_r,
    raw, zl_hi, zl_lo, core_z, streams, k_hi, k_lo, e_hi, e_lo, acc, den_acc, id_col, ids_int, ids, r_ids, id_rows,
    inv_row, r_inv, inv_rows, diag,
    load_sem, direct_send, direct_recv, fwd_send, fwd_recv, core_send, core_recv, ids_send, ids_recv, den_send, den_recv,
):
    blk, grp = lax.axis_index("blk"), lax.axis_index("grp")
    x1 = (flip(blk, 2), grp)
    x3 = (flip(blk, 2), flip(grp, 1))
    y1 = (blk, flip(grp, 2))
    y3 = (blk, flip(flip(grp, 2), 4))
    core = (flip(blk, 1), grp)
    x2 = (blk, flip(grp, 1))
    y2 = (blk, flip(grp, 4))
    partners = (x1, y1, x2, y2, core)

    barrier = pltpu.get_barrier_semaphore()
    for peer in (x1, x3, y1, y3, core, x2, y2):
        pl.semaphore_signal(barrier, inc=1, device_id=peer, device_id_type=MESH)

    loads = [
        pltpu.make_async_copy(one_hbm, raw.at[pl.ds(0, R)], load_sem.at[0]),
        pltpu.make_async_copy(two_hbm, raw.at[pl.ds(R, R)], load_sem.at[1]),
        pltpu.make_async_copy(ids_hbm, ids_int, load_sem.at[2]),
    ]
    for copy in loads:
        copy.start()

    def piece(c, stream):
        return streams.at[c // 2, stream, pl.ds(CR * (c % 2), CR)]

    def direct(axis, c):
        return pltpu.make_async_remote_copy(
            src_ref=z.at[pl.ds(CR * c, CR)],
            dst_ref=piece(c, axis),
            send_sem=direct_send.at[axis, c],
            recv_sem=direct_recv.at[axis, c],
            device_id=(x1, y1)[axis],
            device_id_type=MESH,
        )

    def forward(axis, c):
        return pltpu.make_async_remote_copy(
            src_ref=piece(c, axis),
            dst_ref=piece(c, 2 + axis),
            send_sem=fwd_send.at[axis, c],
            recv_sem=fwd_recv.at[axis, c],
            device_id=(x3, y3)[axis],
            device_id_type=MESH,
        )

    to_core = pltpu.make_async_remote_copy(
        src_ref=z, dst_ref=core_z, send_sem=core_send, recv_sem=core_recv, device_id=core, device_id_type=MESH
    )

    def send_ids(p):
        return pltpu.make_async_remote_copy(
            src_ref=ids, dst_ref=r_ids.at[p], send_sem=ids_send.at[p], recv_sem=ids_recv.at[p],
            device_id=partners[p], device_id_type=MESH,
        )

    def send_inv(p):
        return pltpu.make_async_remote_copy(
            src_ref=inv_row, dst_ref=r_inv.at[p], send_sem=den_send.at[p], recv_sem=den_recv.at[p],
            device_id=partners[p], device_id_type=MESH,
        )

    def normalise(first, count):
        rows = pl.ds(first, count)
        x = raw[rows]
        ir = lax.rsqrt(jnp.sum(x * x, axis=1, keepdims=True) + 1e-06)
        inv_r[rows] = ir
        z[rows] = x * ir

    def launch(c):
        direct(0, c).start()
        direct(1, c).start()

    loads[0].wait()
    normalise(0, 2 * CR)
    pl.semaphore_wait(barrier, 7)
    launch(0)
    normalise(2 * CR, R - 2 * CR)
    launch(1)
    loads[1].wait()
    loads[2].wait()
    for q in range(4):
        ids[pl.ds(2 * q, 2)] = ids_int[...].astype(F32)
    for p in range(5):
        send_ids(p).start()
    normalise(R, R)
    launch(2)

    hi, lo = split(z[...] * LOGIT)
    zl_hi[...] = hi
    zl_lo[...] = lo
    d = jnp.exp2(LOGIT * jnp.sum(z[pl.ds(0, R)] * z[pl.ds(R, R)], axis=1, keepdims=True))
    diag[...] = d
    lane = lax.broadcasted_iota(jnp.int32, (R, 128), 1)
    start = jnp.where(lane == 0, d, 0.0)
    den_acc[pl.ds(0, R)] = start
    den_acc[pl.ds(R, R)] = start
    for q in range(2):
        id_col[pl.ds(128 * q, 128)] = jnp.broadcast_to(ids[pl.ds(q, 1)], (128, 128)).T

    def scores(slot, keys, key_ids):
        place = pl.ds(pl.multiple_of(256 * slot, 256), 256)
        khi, klo = split(keys)
        k_hi[place] = khi
        k_lo[place] = klo
        keep = jnp.concatenate([id_col[...], id_col[...]], axis=1) != key_ids
        s = dot_t(zl_hi[...], khi) + dot_t(zl_hi[...], klo) + dot_t(zl_lo[...], khi)
        e = jnp.where(jnp.concatenate([keep, keep], axis=0), jnp.exp2(s), 0.0)
        den_acc[...] += e[:, :128] + e[:, 128:]
        ehi, elo = split(e)
        e_hi[:, place] = ehi
        e_lo[:, place] = elo

    def gather(first, count):
        place = pl.ds(256 * first, 256 * count)
        part = dot(e_hi[:, place], k_hi[place]) + dot(e_hi[:, place], k_lo[place]) + dot(e_lo[:, place], k_hi[place])
        acc[...] = part if first == 0 else acc[...] + part

    def pair_ids(ref):
        return jnp.concatenate([ref[pl.ds(0, 1)], ref[pl.ds(1, 1)]], axis=1)

    def pass_on(c):
        for axis in range(2):
            direct(axis, c).wait_recv()
            forward(axis, c).start()

        def refill():
            for axis in range(2):
                direct(axis, c).wait_send()
                direct(axis, c + WINDOW).start()

        if isinstance(c, int):
            refill()
        else:
            pl.when(c + WINDOW < CHUNKS)(refill)

    launch(3)
    own_ids = pair_ids(ids)
    scores(0, z[pl.ds(0, R)], own_ids)
    launch(4)
    to_core.start()
    scores(1, z[pl.ds(R, R)], own_ids)
    launch(5)
    pass_on(0)
    pass_on(1)
    for p in range(5):
        send_ids(p).wait_recv()
    to_core.wait_recv()
    core_ids = pair_ids(r_ids.at[4])
    scores(2, core_z[pl.ds(0, R)], core_ids)
    pass_on(2)
    pass_on(3)
    scores(3, core_z[pl.ds(R, R)], core_ids)

    left = lax.broadcasted_iota(jnp.int32, (8, 128), 1) < 64

    def mixed(refs):
        a, b, c, d = (refs[p] for p in range(4))
        turn = lambda x: pltpu.roll(x, 64, 1)
        first = jnp.concatenate([jnp.where(left, a, turn(b)), jnp.where(left, c, turn(d))], axis=1)
        second = jnp.concatenate([jnp.where(left, turn(a), b), jnp.where(left, turn(c), d)], axis=1)
        return first, second

    first, second = mixed(r_ids)
    for q in range(2):
        id_rows[pl.ds(2 * q, 1)] = first[q : q + 1]
        id_rows[pl.ds(2 * q + 1, 1)] = second[q : q + 1]

    def stream_scores(p):
        for axis in range(2):
            forward(axis, 2 * p).wait_recv()
            forward(axis, 2 * p + 1).wait_recv()
        scores(4 + p, streams[p].reshape(8 * CR, D), id_rows[pl.ds(p % 4, 1)])

    def stream_step(p, carry):
        pass_on(2 * p)
        pass_on(2 * p + 1)
        stream_scores(p - 2)
        return carry

    pass_on(4)
    pass_on(5)
    gather(0, 4)
    stream_scores(0)
    lax.fori_loop(3, PAIRS, stream_step, 0)
    stream_scores(PAIRS - 2)
    gather(4, 6)
    stream_scores(PAIRS - 1)

    s_hi = den_acc[...].astype(BF16)
    rest = den_acc[...] - s_hi.astype(F32)
    s_mid, s_lo = split(rest)
    ones = jnp.ones((8, 128), BF16)
    sums = dot_t(ones, s_hi) + dot_t(ones, s_mid) + dot_t(ones, s_lo)
    own_inv = 1.0 / sums
    for q in range(4):
        inv_row[pl.ds(q, 1)] = own_inv[0:1, 128 * q : 128 * (q + 1)]
    for q in range(4):
        inv_row[pl.ds(4 + q, 1)] = own_inv[0:1, 128 * q : 128 * (q + 1)]
    for p in range(5):
        send_inv(p).start()

    gather(10, 2)
    centre = jnp.mean(own_inv[0:1], axis=1, keepdims=True)
    inv_col = 1.0 / jnp.sum(den_acc[...], axis=1, keepdims=True)
    coef = diag[...] * (inv_col[:R] + inv_col[R:]) - 1.0 / TAU
    for h in range(2):
        rows, others = pl.ds(R * h, R), pl.ds(R * (1 - h), R)
        acc[rows] = (inv_col[R * h : R * (h + 1)] + centre) * acc[rows] + coef * z[others]

    for p in range(5):
        send_inv(p).wait_recv()
    first, second = mixed(r_inv)

    def spread(slot, row, lane, values):
        inv_rows[:, pl.ds(256 * slot + lane, values.shape[1])] = jnp.broadcast_to(values[row : row + 1] - centre, (16, values.shape[1])).astype(BF16)

    own, other = inv_row[...], r_inv[4]
    for q in range(4):
        spread(q // 2, q, 128 * (q % 2), own)
        spread(2 + q // 2, q, 128 * (q % 2), other)
        spread(4 + 2 * q, q, 0, first)
        spread(5 + 2 * q, q, 0, second)

    for h in range(2):
        rows = pl.ds(R * h, R)
        weight = jnp.broadcast_to(inv_rows[0:1], (R, 256 * STEPS))
        grad[rows] = acc[rows] + dot(e_hi[rows] * weight, k_hi[...])

    for c in range(CHUNKS):
        for axis in range(2):
            if c >= CHUNKS - WINDOW:
                direct(axis, c).wait_send()
            forward(axis, c).wait_send()
    to_core.wait_send()
    for p in range(5):
        send_ids(p).wait_send()
        send_inv(p).wait_send()


def finish(z, grad, inv_r, out_one, out_two, result, out_sem):
    outs = []
    for c in range(4):
        rows = pl.ds(128 * c, 128)
        g, own = grad[rows], z[rows]
        result[rows] = (g - own * jnp.sum(own * g, axis=1, keepdims=True)) * inv_r[rows]
        copy = pltpu.make_async_copy(
            result.at[rows], (out_one, out_two)[c // 2].at[pl.ds(128 * (c % 2), 128)], out_sem.at[c]
        )
        copy.start()
        outs.append(copy)
    for copy in outs:
        copy.wait()


def on_device(view_one, view_two, node_ids):
    dma = pltpu.SemaphoreType.DMA
    hbm = pl.BlockSpec(memory_space=pltpu.HBM)
    vmem = pl.BlockSpec(memory_space=pltpu.VMEM)
    middle = pl.pallas_call(
        kernel,
        out_shape=(
            pltpu.VMEM((2 * R, D), F32),
            pltpu.VMEM((2 * R, D), F32),
            pltpu.VMEM((2 * R, 1), F32),
        ),
        in_specs=[hbm] * 3,
        out_specs=(vmem,) * 3,
        scratch_shapes=[
            pltpu.VMEM((2 * R, D), F32),
            pltpu.VMEM((2 * R, D), BF16),
            pltpu.VMEM((2 * R, D), BF16),
            pltpu.VMEM((2 * R, D), F32),
            pltpu.VMEM((PAIRS, 4, 2 * CR, D), F32),
            pltpu.VMEM((256 * STEPS, D), BF16),
            pltpu.VMEM((256 * STEPS, D), BF16),
            pltpu.VMEM((2 * R, 256 * STEPS), BF16),
            pltpu.VMEM((2 * R, 256 * STEPS), BF16),
            pltpu.VMEM((2 * R, D), F32),
            pltpu.VMEM((2 * R, 128), F32),
            pltpu.VMEM((R, 128), F32),
            pltpu.VMEM((2, 128), jnp.int32),
            pltpu.VMEM((8, 128), F32),
            pltpu.VMEM((5, 8, 128), F32),
            pltpu.VMEM((8, 256), F32),
            pltpu.VMEM((8, 128), F32),
            pltpu.VMEM((5, 8, 128), F32),
            pltpu.VMEM((16, 256 * STEPS), BF16),
            pltpu.VMEM((R, 1), F32),
            dma((3,)),
            dma((2, CHUNKS)),
            dma((2, CHUNKS)),
            dma((2, CHUNKS)),
            dma((2, CHUNKS)),
            dma,
            dma,
            dma((5,)),
            dma((5,)),
            dma((5,)),
            dma((5,)),
        ],
        compiler_params=pltpu.CompilerParams(
            collective_id=0, has_side_effects=True, vmem_limit_bytes=32 * 1024 * 1024
        ),
    )(*(pltpu.with_memory_space_constraint(x, pltpu.HBM) for x in (view_one, view_two, node_ids.reshape(2, 128))))
    return pl.pallas_call(
        finish,
        out_shape=(jax.ShapeDtypeStruct((R, D), F32), jax.ShapeDtypeStruct((R, D), F32)),
        in_specs=[vmem] * 3,
        out_specs=(hbm, hbm),
        scratch_shapes=[pltpu.VMEM((2 * R, D), F32), dma((4,))],
        compiler_params=pltpu.CompilerParams(vmem_limit_bytes=4 * 1024 * 1024),
    )(*middle)


def solution(mesh):
    rows = P(("blk", "grp"), None)
    return jax.shard_map(
        on_device,
        mesh=mesh,
        in_specs=(rows, rows, P(("blk", "grp"))),
        out_specs=(rows, rows),
        check_vma=False,
    )
```

```python
import math

import jax
import jax.numpy as jnp
from jax import lax
from jax.experimental import pallas as pl
from jax.experimental.pallas import tpu as pltpu
from jax.sharding import PartitionSpec as P

MESH = pl.DeviceIdType.MESH
F32, BF16 = jnp.float32, jnp.bfloat16

R = 256
D = 256
CHUNKS = 8
CR = 2 * R // CHUNKS
TAU = 0.5
LOGIT = 1.0 / (TAU * math.log(2.0))
WINDOW = 3
STEPS = 12


def flip(n, bit):
    return n + bit - 2 * bit * ((n // bit) % 2)


def split(x):
    hi = x.astype(BF16)
    return hi, (x - hi.astype(F32)).astype(BF16)


def dot_t(a, b):
    return lax.dot_general(a, b, (((1,), (1,)), ((), ())), preferred_element_type=F32)


def dot(a, b):
    return lax.dot_general(a, b, (((1,), (0,)), ((), ())), preferred_element_type=F32)


def kernel(
    one_hbm, two_hbm, ids_hbm, z, grad, inv_r,
    raw, zl, core_z, streams, keys_all, e_all, acc, key_sum, den_acc, id_col, ids_int, ids, r_ids, id_rows,
    inv_row, r_inv, inv_rows, diag,
    load_sem, direct_send, direct_recv, fwd_send, fwd_recv, core_send, core_recv, ids_send, ids_recv, den_send, den_recv,
):
    blk, grp = lax.axis_index("blk"), lax.axis_index("grp")
    x1 = (flip(blk, 2), grp)
    x3 = (flip(blk, 2), flip(grp, 1))
    y1 = (blk, flip(grp, 2))
    y3 = (blk, flip(flip(grp, 2), 4))
    core = (flip(blk, 1), grp)
    x2 = (blk, flip(grp, 1))
    y2 = (blk, flip(grp, 4))
    partners = (x1, y1, x2, y2, core)

    barrier = pltpu.get_barrier_semaphore()
    for peer in (x1, x3, y1, y3, core, x2, y2):
        pl.semaphore_signal(barrier, inc=1, device_id=peer, device_id_type=MESH)

    loads = [
        pltpu.make_async_copy(one_hbm, raw.at[pl.ds(0, R)], load_sem.at[0]),
        pltpu.make_async_copy(two_hbm, raw.at[pl.ds(R, R)], load_sem.at[1]),
        pltpu.make_async_copy(ids_hbm, ids_int, load_sem.at[2]),
    ]
    for copy in loads:
        copy.start()

    def direct(axis, c):
        return pltpu.make_async_remote_copy(
            src_ref=z.at[pl.ds(CR * c, CR)],
            dst_ref=streams.at[c, axis],
            send_sem=direct_send.at[axis],
            recv_sem=direct_recv.at[axis, c],
            device_id=(x1, y1)[axis],
            device_id_type=MESH,
        )

    def forward(axis, c):
        return pltpu.make_async_remote_copy(
            src_ref=streams.at[c, axis],
            dst_ref=streams.at[c, 2 + axis],
            send_sem=fwd_send.at[axis],
            recv_sem=fwd_recv.at[axis, c],
            device_id=(x3, y3)[axis],
            device_id_type=MESH,
        )

    def to_core(h):
        rows = pl.ds(R * h, R)
        return pltpu.make_async_remote_copy(
            src_ref=z.at[rows], dst_ref=core_z.at[rows], send_sem=core_send, recv_sem=core_recv.at[h],
            device_id=core, device_id_type=MESH,
        )

    def whole(ref, send, recv):
        return pltpu.make_async_remote_copy(
            src_ref=ref, dst_ref=ref, send_sem=send, recv_sem=recv, device_id=core, device_id_type=MESH
        )

    def send_ids(p):
        return pltpu.make_async_remote_copy(
            src_ref=ids, dst_ref=r_ids.at[p], send_sem=ids_send, recv_sem=ids_recv,
            device_id=partners[p], device_id_type=MESH,
        )

    def send_inv(p):
        return pltpu.make_async_remote_copy(
            src_ref=inv_row, dst_ref=r_inv.at[p], send_sem=den_send, recv_sem=den_recv,
            device_id=partners[p], device_id_type=MESH,
        )

    def normalise(first, count):
        rows = pl.ds(first, count)
        x = raw[rows]
        ir = lax.rsqrt(jnp.sum(x * x, axis=1, keepdims=True) + 1e-06)
        inv_r[rows] = ir
        z[rows] = x * ir

    def launch(c):
        direct(0, c).start()
        direct(1, c).start()

    loads[0].wait()
    normalise(0, CR)
    pl.semaphore_wait(barrier, 7)
    launch(0)
    normalise(CR, R - CR)
    to_core(0).start()
    loads[1].wait()
    loads[2].wait()
    for q in range(4):
        ids[pl.ds(2 * q, 2)] = ids_int[...].astype(F32)
    for p in range(5):
        send_ids(p).start()
    normalise(R, R)
    launch(1)
    to_core(1).start()

    zl[...] = (z[...] * LOGIT).astype(BF16)
    d = jnp.exp2(LOGIT * jnp.sum(z[pl.ds(0, R)] * z[pl.ds(R, R)], axis=1, keepdims=True))
    diag[...] = d
    lane = lax.broadcasted_iota(jnp.int32, (R, 128), 1)
    start = jnp.where(lane == 0, d, 0.0)
    den_acc[pl.ds(0, R)] = start
    den_acc[pl.ds(R, R)] = start
    key_sum[...] = jnp.zeros_like(key_sum)
    for q in range(2):
        id_col[pl.ds(128 * q, 128)] = jnp.broadcast_to(ids[pl.ds(q, 1)], (128, 128)).T

    def scores(slot, keys, key_ids):
        place = pl.ds(pl.multiple_of(256 * slot, 256), 256)
        narrow = keys.astype(BF16)
        keys_all[place] = narrow
        key_sum[...] += jnp.sum(keys.reshape(32, 8, D), axis=0)
        keep = jnp.concatenate([id_col[...], id_col[...]], axis=1) != key_ids
        e = jnp.where(jnp.concatenate([keep, keep], axis=0), jnp.exp2(dot_t(zl[...], narrow)), 0.0)
        den_acc[...] += e[:, :128] + e[:, 128:]
        e_all[:, place] = (e - 1.0).astype(BF16)

    def gather(group):
        place = pl.ds(1024 * group, 1024)
        part = dot(e_all[:, place], keys_all[place])
        acc[...] = part if group == 0 else acc[...] + part

    def pair_ids(ref):
        return jnp.concatenate([ref[pl.ds(0, 1)], ref[pl.ds(1, 1)]], axis=1)

    def pass_on(c):
        for axis in range(2):
            direct(axis, c).wait_recv()
            forward(axis, c).start()
        if isinstance(c, int):
            launch(c + WINDOW)
        else:
            pl.when(c + WINDOW < CHUNKS)(lambda: launch(c + WINDOW))

    own_ids = pair_ids(ids)
    scores(0, z[pl.ds(0, R)], own_ids)
    launch(2)
    scores(1, z[pl.ds(R, R)], own_ids)
    pass_on(0)
    whole(r_ids, ids_send, ids_recv).wait_recv()
    core_ids = pair_ids(r_ids.at[4])
    to_core(0).wait_recv()
    scores(2, core_z[pl.ds(0, R)], core_ids)
    pass_on(1)
    to_core(1).wait_recv()
    scores(3, core_z[pl.ds(R, R)], core_ids)
    gather(0)

    left = lax.broadcasted_iota(jnp.int32, (8, 128), 1) < 64

    def mixed(refs):
        a, b, c, d = (refs[p] for p in range(4))
        turn = lambda x: pltpu.roll(x, 64, 1)
        first = jnp.concatenate([jnp.where(left, a, turn(b)), jnp.where(left, c, turn(d))], axis=1)
        second = jnp.concatenate([jnp.where(left, turn(a), b), jnp.where(left, turn(c), d)], axis=1)
        return first, second

    first, second = mixed(r_ids)
    for q in range(2):
        id_rows[pl.ds(2 * q, 1)] = first[q : q + 1]
        id_rows[pl.ds(2 * q + 1, 1)] = second[q : q + 1]

    def arrived(c):
        for axis in range(2):
            forward(axis, c).wait_recv()

    def stream_scores(c):
        scores(4 + c, streams[c].reshape(4 * CR, D), id_rows[pl.ds(c % 4, 1)])

    def stream_step(c, carry):
        pass_on(c + 2)
        arrived(c)
        stream_scores(c)
        return carry

    lax.fori_loop(0, 4, stream_step, 0)
    gather(1)
    lax.fori_loop(4, CHUNKS - 2, stream_step, 0)
    for c in range(CHUNKS - 2, CHUNKS):
        arrived(c)
        stream_scores(c)

    s_hi = den_acc[...].astype(BF16)
    rest = den_acc[...] - s_hi.astype(F32)
    s_mid, s_lo = split(rest)
    ones = jnp.ones((8, 128), BF16)
    sums = dot_t(ones, s_hi) + dot_t(ones, s_mid) + dot_t(ones, s_lo)
    own_inv = 1.0 / sums
    for q in range(4):
        inv_row[pl.ds(q, 1)] = own_inv[0:1, 128 * q : 128 * (q + 1)]
    for q in range(4):
        inv_row[pl.ds(4 + q, 1)] = own_inv[0:1, 128 * q : 128 * (q + 1)]
    for p in range(5):
        send_inv(p).start()

    gather(2)
    centre = jnp.mean(own_inv[0:1], axis=1, keepdims=True)
    inv_col = 1.0 / jnp.sum(den_acc[...], axis=1, keepdims=True)
    coef = diag[...] * (inv_col[:R] + inv_col[R:]) - 1.0 / TAU
    for h in range(2):
        rows, others = pl.ds(R * h, R), pl.ds(R * (1 - h), R)
        total = acc[rows] + jnp.sum(key_sum[...], axis=0, keepdims=True)
        acc[rows] = (inv_col[R * h : R * (h + 1)] + centre) * total + coef * z[others]

    def spread(slot, row, lane, values):
        inv_rows[0:1, pl.ds(256 * slot + lane, values.shape[1])] = values[row : row + 1] - centre

    def weighted(first, count):
        place = pl.ds(256 * first, 256 * count)
        off = jnp.broadcast_to(inv_rows[0:1, place], (16, 256 * count)).astype(BF16)[None]
        e = e_all[:, place].reshape(2 * R // 16, 16, 256 * count)
        return dot((e * off + off).reshape(2 * R, 256 * count), keys_all[place])

    own = inv_row[...]
    for q in range(4):
        spread(q // 2, q, 128 * (q % 2), own)
    acc[...] += weighted(0, 2)

    whole(r_inv, den_send, den_recv).wait_recv()
    first, second = mixed(r_inv)
    other = r_inv[4]
    for q in range(4):
        spread(2 + q // 2, q, 128 * (q % 2), other)
        spread(4 + 2 * q, q, 0, first)
        spread(5 + 2 * q, q, 0, second)
    grad[...] = acc[...] + weighted(2, STEPS - 2)

    for axis in range(2):
        whole(z, direct_send.at[axis], core_recv.at[0]).wait_send()
        whole(z, fwd_send.at[axis], core_recv.at[0]).wait_send()
    whole(z, core_send, core_recv.at[0]).wait_send()
    whole(r_ids, ids_send, ids_recv).wait_send()
    whole(r_inv, den_send, den_recv).wait_send()


def finish(z, grad, inv_r, out_one, out_two, result, out_sem):
    outs = []
    for c in range(4):
        rows = pl.ds(128 * c, 128)
        g, own = grad[rows], z[rows]
        result[rows] = (g - own * jnp.sum(own * g, axis=1, keepdims=True)) * inv_r[rows]
        copy = pltpu.make_async_copy(
            result.at[rows], (out_one, out_two)[c // 2].at[pl.ds(128 * (c % 2), 128)], out_sem.at[c]
        )
        copy.start()
        outs.append(copy)
    for copy in outs:
        copy.wait()


def on_device(view_one, view_two, node_ids):
    dma = pltpu.SemaphoreType.DMA
    hbm = pl.BlockSpec(memory_space=pltpu.HBM)
    vmem = pl.BlockSpec(memory_space=pltpu.VMEM)
    middle = pl.pallas_call(
        kernel,
        out_shape=(
            pltpu.VMEM((2 * R, D), F32),
            pltpu.VMEM((2 * R, D), F32),
            pltpu.VMEM((2 * R, 1), F32),
        ),
        in_specs=[hbm] * 3,
        out_specs=(vmem,) * 3,
        scratch_shapes=[
            pltpu.VMEM((2 * R, D), F32),
            pltpu.VMEM((2 * R, D), BF16),
            pltpu.VMEM((2 * R, D), F32),
            pltpu.VMEM((CHUNKS, 4, CR, D), F32),
            pltpu.VMEM((256 * STEPS, D), BF16),
            pltpu.VMEM((2 * R, 256 * STEPS), BF16),
            pltpu.VMEM((2 * R, D), F32),
            pltpu.VMEM((8, D), F32),
            pltpu.VMEM((2 * R, 128), F32),
            pltpu.VMEM((R, 128), F32),
            pltpu.VMEM((2, 128), jnp.int32),
            pltpu.VMEM((8, 128), F32),
            pltpu.VMEM((5, 8, 128), F32),
            pltpu.VMEM((8, 256), F32),
            pltpu.VMEM((8, 128), F32),
            pltpu.VMEM((5, 8, 128), F32),
            pltpu.VMEM((8, 256 * STEPS), F32),
            pltpu.VMEM((R, 1), F32),
            dma((3,)),
            dma((2,)),
            dma((2, CHUNKS)),
            dma((2,)),
            dma((2, CHUNKS)),
            dma,
            dma((2,)),
            dma,
            dma,
            dma,
            dma,
        ],
        compiler_params=pltpu.CompilerParams(
            collective_id=0, has_side_effects=True, vmem_limit_bytes=32 * 1024 * 1024
        ),
    )(*(pltpu.with_memory_space_constraint(x, pltpu.HBM) for x in (view_one, view_two, node_ids.reshape(2, 128))))
    return pl.pallas_call(
        finish,
        out_shape=(jax.ShapeDtypeStruct((R, D), F32), jax.ShapeDtypeStruct((R, D), F32)),
        in_specs=[vmem] * 3,
        out_specs=(hbm, hbm),
        scratch_shapes=[pltpu.VMEM((2 * R, D), F32), dma((4,))],
        compiler_params=pltpu.CompilerParams(vmem_limit_bytes=4 * 1024 * 1024),
    )(*middle)


def solution(mesh):
    rows = P(("blk", "grp"), None)
    return jax.shard_map(
        on_device,
        mesh=mesh,
        in_specs=(rows, rows, P(("blk", "grp"))),
        out_specs=(rows, rows),
        check_vma=False,
    )
```

```python
import math

import jax
import jax.numpy as jnp
from jax import lax
from jax.experimental import pallas as pl
from jax.experimental.pallas import tpu as pltpu
from jax.sharding import PartitionSpec as P

MESH = pl.DeviceIdType.MESH
F32, BF16 = jnp.float32, jnp.bfloat16

R = 256
D = 256
CHUNKS = 8
CR = 2 * R // CHUNKS
TAU = 0.5
LOGIT = 1.0 / (TAU * math.log(2.0))
STEPS = 12


def flip(n, bit):
    return n + bit - 2 * bit * ((n // bit) % 2)


def split(x):
    hi = x.astype(BF16)
    return hi, (x - hi.astype(F32)).astype(BF16)


def dot_t(a, b):
    return lax.dot_general(a, b, (((1,), (1,)), ((), ())), preferred_element_type=F32)


def dot(a, b):
    return lax.dot_general(a, b, (((1,), (0,)), ((), ())), preferred_element_type=F32)


def kernel(
    one_hbm, two_hbm, ids_hbm, z, grad, inv_r,
    raw, zl, core_z, streams, keys_all, e_all, acc, key_sum, den_acc, id_col, ids_int, ids, r_ids, id_rows,
    inv_row, r_inv, inv_rows, diag,
    load_sem, direct_send, direct_recv, fwd_send, fwd_recv, core_send, core_recv, ids_send, ids_recv, den_send, den_recv,
):
    blk, grp = lax.axis_index("blk"), lax.axis_index("grp")
    x1 = (flip(blk, 2), grp)
    x3 = (flip(blk, 2), flip(grp, 1))
    y1 = (blk, flip(grp, 2))
    y3 = (blk, flip(flip(grp, 2), 4))
    core = (flip(blk, 1), grp)
    x2 = (blk, flip(grp, 1))
    y2 = (blk, flip(grp, 4))
    partners = (x1, y1, x2, y2, core)

    barrier = pltpu.get_barrier_semaphore()
    for peer in (x1, x3, y1, y3, core):
        pl.semaphore_signal(barrier, inc=1, device_id=peer, device_id_type=MESH)

    loads = [
        pltpu.make_async_copy(one_hbm, raw.at[pl.ds(0, R)], load_sem.at[0]),
        pltpu.make_async_copy(two_hbm, raw.at[pl.ds(R, R)], load_sem.at[1]),
        pltpu.make_async_copy(ids_hbm, ids_int, load_sem.at[2]),
    ]
    for copy in loads:
        copy.start()

    def direct(axis, c, first=0, count=CR, sem=None):
        return pltpu.make_async_remote_copy(
            src_ref=z.at[pl.ds(CR * c + first, count)],
            dst_ref=streams.at[c, axis, pl.ds(first, count)],
            send_sem=direct_send.at[axis],
            recv_sem=direct_recv.at[axis, c if sem is None else sem],
            device_id=(x1, y1)[axis],
            device_id_type=MESH,
        )

    def forward(axis, c, first=0, count=CR, sem=None):
        return pltpu.make_async_remote_copy(
            src_ref=streams.at[c, axis, pl.ds(first, count)],
            dst_ref=streams.at[c, 2 + axis, pl.ds(first, count)],
            send_sem=fwd_send.at[axis],
            recv_sem=fwd_recv.at[axis, c if sem is None else sem],
            device_id=(x3, y3)[axis],
            device_id_type=MESH,
        )

    last = [(CHUNKS - 1, 0, CR // 2, CHUNKS - 1), (CHUNKS - 1, CR // 2, CR // 2, CHUNKS)]

    def to_core(h):
        rows = pl.ds(R * h, R)
        return pltpu.make_async_remote_copy(
            src_ref=z.at[rows], dst_ref=core_z.at[rows], send_sem=core_send, recv_sem=core_recv.at[h],
            device_id=core, device_id_type=MESH,
        )

    def whole(ref, send, recv):
        return pltpu.make_async_remote_copy(
            src_ref=ref, dst_ref=ref, send_sem=send, recv_sem=recv, device_id=core, device_id_type=MESH
        )

    def send_ids(p):
        return pltpu.make_async_remote_copy(
            src_ref=ids, dst_ref=r_ids.at[p], send_sem=ids_send, recv_sem=ids_recv.at[p],
            device_id=partners[p], device_id_type=MESH,
        )

    def forward_ids(axis):
        return pltpu.make_async_remote_copy(
            src_ref=r_ids.at[axis], dst_ref=r_ids.at[2 + axis], send_sem=ids_send, recv_sem=ids_recv.at[2 + axis],
            device_id=(x3, y3)[axis], device_id_type=MESH,
        )

    def send_inv(p):
        return pltpu.make_async_remote_copy(
            src_ref=inv_row, dst_ref=r_inv.at[p], send_sem=den_send, recv_sem=den_recv,
            device_id=partners[p], device_id_type=MESH,
        )

    def normalise(first, count):
        rows = pl.ds(first, count)
        x = raw[rows]
        ir = lax.rsqrt(jnp.sum(x * x, axis=1, keepdims=True) + 1e-06)
        inv_r[rows] = ir
        z[rows] = x * ir

    def launch(*piece):
        direct(0, *piece).start()
        direct(1, *piece).start()

    loads[0].wait()
    normalise(0, CR)
    loads[2].wait()
    for q in range(4):
        ids[pl.ds(2 * q, 2)] = ids_int[...].astype(F32)
    pl.semaphore_wait(barrier, 5)
    launch(0)
    for p in (0, 1, 4):
        send_ids(p).start()
    normalise(CR, R - CR)
    for c in range(1, CHUNKS // 2):
        launch(c)
    to_core(0).start()
    loads[1].wait()
    normalise(R, R)
    for c in range(CHUNKS // 2, CHUNKS - 1):
        launch(c)
    for piece in last:
        launch(*piece)
    to_core(1).start()

    zl[...] = (z[...] * LOGIT).astype(BF16)
    d = jnp.exp2(LOGIT * jnp.sum(z[pl.ds(0, R)] * z[pl.ds(R, R)], axis=1, keepdims=True))
    diag[...] = d
    lane = lax.broadcasted_iota(jnp.int32, (R, 128), 1)
    start = jnp.where(lane == 0, d, 0.0)
    den_acc[pl.ds(0, R)] = start
    den_acc[pl.ds(R, R)] = start
    key_sum[...] = jnp.zeros_like(key_sum)
    for q in range(2):
        id_col[pl.ds(128 * q, 128)] = jnp.broadcast_to(ids[pl.ds(q, 1)], (128, 128)).T

    def scores(slot, keys, key_ids):
        place = pl.ds(pl.multiple_of(256 * slot, 256), 256)
        narrow = keys.astype(BF16)
        keys_all[place] = narrow
        key_sum[...] += jnp.sum(keys.reshape(32, 8, D), axis=0)
        keep = jnp.concatenate([id_col[...], id_col[...]], axis=1) != key_ids
        e = jnp.where(jnp.concatenate([keep, keep], axis=0), jnp.exp2(dot_t(zl[...], narrow)), 0.0)
        den_acc[...] += e[:, :128] + e[:, 128:]
        e_all[:, place] = (e - 1.0).astype(BF16)

    def gather(group):
        place = pl.ds(1024 * group, 1024)
        part = dot(e_all[:, place], keys_all[place])
        acc[...] = part if group == 0 else acc[...] + part

    def pair_ids(ref):
        return jnp.concatenate([ref[pl.ds(0, 1)], ref[pl.ds(1, 1)]], axis=1)

    def pass_on(*piece):
        for axis in range(2):
            direct(axis, *piece).wait_recv()
            forward(axis, *piece).start()

    own_ids = pair_ids(ids)
    scores(0, z[pl.ds(0, R)], own_ids)
    pass_on(0)
    for axis in range(2):
        send_ids(axis).wait_recv()
        forward_ids(axis).start()
    scores(1, z[pl.ds(R, R)], own_ids)
    pass_on(1)
    send_ids(4).wait_recv()
    core_ids = pair_ids(r_ids.at[4])
    to_core(0).wait_recv()
    scores(2, core_z[pl.ds(0, R)], core_ids)
    pass_on(2)
    to_core(1).wait_recv()
    scores(3, core_z[pl.ds(R, R)], core_ids)
    pass_on(3)
    gather(0)
    for axis in range(2):
        forward_ids(axis).wait_recv()

    left = lax.broadcasted_iota(jnp.int32, (8, 128), 1) < 64

    def mixed(refs):
        a, b, c, d = (refs[p] for p in range(4))
        turn = lambda x: pltpu.roll(x, 64, 1)
        first = jnp.concatenate([jnp.where(left, a, turn(b)), jnp.where(left, c, turn(d))], axis=1)
        second = jnp.concatenate([jnp.where(left, turn(a), b), jnp.where(left, turn(c), d)], axis=1)
        return first, second

    first, second = mixed(r_ids)
    for q in range(2):
        id_rows[pl.ds(2 * q, 1)] = first[q : q + 1]
        id_rows[pl.ds(2 * q + 1, 1)] = second[q : q + 1]

    def stream_scores(c, pieces):
        for piece in pieces:
            for axis in range(2):
                forward(axis, *piece).wait_recv()
        scores(4 + c, streams[c].reshape(4 * CR, D), id_rows[pl.ds(c % 4, 1)])

    def stream_step(c, carry):
        stream_scores(c, [(c,)])
        pass_on(c + 4)
        return carry

    lax.fori_loop(0, CHUNKS - 5, stream_step, 0)
    stream_scores(CHUNKS - 5, [(CHUNKS - 5,)])
    pass_on(*last[0])
    pass_on(*last[1])
    for c in range(CHUNKS - 4, CHUNKS - 1):
        stream_scores(c, [(c,)])
    stream_scores(CHUNKS - 1, last)

    s_hi = den_acc[...].astype(BF16)
    rest = den_acc[...] - s_hi.astype(F32)
    s_mid, s_lo = split(rest)
    ones = jnp.ones((8, 128), BF16)
    sums = dot_t(ones, s_hi) + dot_t(ones, s_mid) + dot_t(ones, s_lo)
    own_inv = 1.0 / sums
    for q in range(4):
        inv_row[pl.ds(q, 1)] = own_inv[0:1, 128 * q : 128 * (q + 1)]
    for q in range(4):
        inv_row[pl.ds(4 + q, 1)] = own_inv[0:1, 128 * q : 128 * (q + 1)]
    for p in range(5):
        send_inv(p).start()

    gather(1)
    gather(2)
    centre = jnp.mean(own_inv[0:1], axis=1, keepdims=True)
    inv_col = 1.0 / jnp.sum(den_acc[...], axis=1, keepdims=True)
    coef = diag[...] * (inv_col[:R] + inv_col[R:]) - 1.0 / TAU
    for h in range(2):
        rows, others = pl.ds(R * h, R), pl.ds(R * (1 - h), R)
        total = acc[rows] + jnp.sum(key_sum[...], axis=0, keepdims=True)
        acc[rows] = (inv_col[R * h : R * (h + 1)] + centre) * total + coef * z[others]

    def spread(slot, row, lane, values):
        inv_rows[0:1, pl.ds(256 * slot + lane, values.shape[1])] = values[row : row + 1] - centre

    def weighted(first, count):
        place = pl.ds(256 * first, 256 * count)
        off = jnp.broadcast_to(inv_rows[0:1, place], (16, 256 * count)).astype(BF16)[None]
        e = e_all[:, place].reshape(2 * R // 16, 16, 256 * count)
        return dot((e * off + off).reshape(2 * R, 256 * count), keys_all[place])

    own = inv_row[...]
    for q in range(4):
        spread(q // 2, q, 128 * (q % 2), own)
    acc[...] += weighted(0, 2)

    whole(r_inv, den_send, den_recv).wait_recv()
    first, second = mixed(r_inv)
    other = r_inv[4]
    for q in range(4):
        spread(2 + q // 2, q, 128 * (q % 2), other)
        spread(4 + 2 * q, q, 0, first)
        spread(5 + 2 * q, q, 0, second)
    grad[...] = acc[...] + weighted(2, STEPS - 2)

    for axis in range(2):
        whole(z, direct_send.at[axis], core_recv.at[0]).wait_send()
        whole(z, fwd_send.at[axis], core_recv.at[0]).wait_send()
    whole(z, core_send, core_recv.at[0]).wait_send()
    whole(r_ids, ids_send, core_recv.at[0]).wait_send()
    whole(r_inv, den_send, core_recv.at[0]).wait_send()


def finish(z, grad, inv_r, out_one, out_two, result, out_sem):
    outs = []
    for c in range(4):
        rows = pl.ds(128 * c, 128)
        g, own = grad[rows], z[rows]
        result[rows] = (g - own * jnp.sum(own * g, axis=1, keepdims=True)) * inv_r[rows]
        copy = pltpu.make_async_copy(
            result.at[rows], (out_one, out_two)[c // 2].at[pl.ds(128 * (c % 2), 128)], out_sem.at[c]
        )
        copy.start()
        outs.append(copy)
    for copy in outs:
        copy.wait()


def on_device(view_one, view_two, node_ids):
    dma = pltpu.SemaphoreType.DMA
    hbm = pl.BlockSpec(memory_space=pltpu.HBM)
    vmem = pl.BlockSpec(memory_space=pltpu.VMEM)
    middle = pl.pallas_call(
        kernel,
        out_shape=(
            pltpu.VMEM((2 * R, D), F32),
            pltpu.VMEM((2 * R, D), F32),
            pltpu.VMEM((2 * R, 1), F32),
        ),
        in_specs=[hbm] * 3,
        out_specs=(vmem,) * 3,
        scratch_shapes=[
            pltpu.VMEM((2 * R, D), F32),
            pltpu.VMEM((2 * R, D), BF16),
            pltpu.VMEM((2 * R, D), F32),
            pltpu.VMEM((CHUNKS, 4, CR, D), F32),
            pltpu.VMEM((256 * STEPS, D), BF16),
            pltpu.VMEM((2 * R, 256 * STEPS), BF16),
            pltpu.VMEM((2 * R, D), F32),
            pltpu.VMEM((8, D), F32),
            pltpu.VMEM((2 * R, 128), F32),
            pltpu.VMEM((R, 128), F32),
            pltpu.VMEM((2, 128), jnp.int32),
            pltpu.VMEM((8, 128), F32),
            pltpu.VMEM((5, 8, 128), F32),
            pltpu.VMEM((8, 256), F32),
            pltpu.VMEM((8, 128), F32),
            pltpu.VMEM((5, 8, 128), F32),
            pltpu.VMEM((8, 256 * STEPS), F32),
            pltpu.VMEM((R, 1), F32),
            dma((3,)),
            dma((2,)),
            dma((2, CHUNKS + 1)),
            dma((2,)),
            dma((2, CHUNKS + 1)),
            dma,
            dma((2,)),
            dma,
            dma((5,)),
            dma,
            dma,
        ],
        compiler_params=pltpu.CompilerParams(
            collective_id=0, has_side_effects=True, vmem_limit_bytes=32 * 1024 * 1024
        ),
    )(*(pltpu.with_memory_space_constraint(x, pltpu.HBM) for x in (view_one, view_two, node_ids.reshape(2, 128))))
    return pl.pallas_call(
        finish,
        out_shape=(jax.ShapeDtypeStruct((R, D), F32), jax.ShapeDtypeStruct((R, D), F32)),
        in_specs=[vmem] * 3,
        out_specs=(hbm, hbm),
        scratch_shapes=[pltpu.VMEM((2 * R, D), F32), dma((4,))],
        compiler_params=pltpu.CompilerParams(vmem_limit_bytes=4 * 1024 * 1024),
    )(*middle)


def solution(mesh):
    rows = P(("blk", "grp"), None)
    return jax.shard_map(
        on_device,
        mesh=mesh,
        in_specs=(rows, rows, P(("blk", "grp"))),
        out_specs=(rows, rows),
        check_vma=False,
    )
```

```python
import math

import jax
import jax.numpy as jnp
from jax import lax
from jax.experimental import pallas as pl
from jax.experimental.pallas import tpu as pltpu
from jax.sharding import PartitionSpec as P

MESH = pl.DeviceIdType.MESH
F32, BF16 = jnp.float32, jnp.bfloat16

R = 256
D = 256
CHUNKS = 8
CR = 2 * R // CHUNKS
TAU = 0.5
LOGIT = 1.0 / (TAU * math.log(2.0))
STEPS = 12


def flip(n, bit):
    return n + bit - 2 * bit * ((n // bit) % 2)


def split(x):
    hi = x.astype(BF16)
    return hi, (x - hi.astype(F32)).astype(BF16)


def dot_t(a, b):
    return lax.dot_general(a, b, (((1,), (1,)), ((), ())), preferred_element_type=F32)


def dot(a, b):
    return lax.dot_general(a, b, (((1,), (0,)), ((), ())), preferred_element_type=F32)


def kernel(
    one_hbm, two_hbm, ids_hbm, z, grad, inv_r,
    raw, zl_hi, zl_lo, core_z, streams, k_hi, k_lo, e_hi, e_lo, acc, den_acc, id_col, ids_int, ids, r_ids, id_rows,
    inv_row, r_inv, inv_rows, diag,
    load_sem, direct_send, direct_recv, fwd_send, fwd_recv, core_send, core_recv, ids_send, ids_recv, den_send, den_recv,
):
    blk, grp = lax.axis_index("blk"), lax.axis_index("grp")
    x1 = (flip(blk, 2), grp)
    x3 = (flip(blk, 2), flip(grp, 1))
    y1 = (blk, flip(grp, 2))
    y3 = (blk, flip(flip(grp, 2), 4))
    core = (flip(blk, 1), grp)
    x2 = (blk, flip(grp, 1))
    y2 = (blk, flip(grp, 4))
    partners = (x1, y1, x2, y2, core)

    barrier = pltpu.get_barrier_semaphore()
    for peer in (x1, x3, y1, y3, core):
        pl.semaphore_signal(barrier, inc=1, device_id=peer, device_id_type=MESH)

    loads = [
        pltpu.make_async_copy(one_hbm, raw.at[pl.ds(0, R)], load_sem.at[0]),
        pltpu.make_async_copy(two_hbm, raw.at[pl.ds(R, R)], load_sem.at[1]),
        pltpu.make_async_copy(ids_hbm, ids_int, load_sem.at[2]),
    ]
    for copy in loads:
        copy.start()

    def direct(axis, c, first=0, count=CR, sem=None):
        return pltpu.make_async_remote_copy(
            src_ref=z.at[pl.ds(CR * c + first, count)],
            dst_ref=streams.at[c, axis, pl.ds(first, count)],
            send_sem=direct_send.at[axis],
            recv_sem=direct_recv.at[axis, c if sem is None else sem],
            device_id=(x1, y1)[axis],
            device_id_type=MESH,
        )

    def forward(axis, c, first=0, count=CR, sem=None):
        return pltpu.make_async_remote_copy(
            src_ref=streams.at[c, axis, pl.ds(first, count)],
            dst_ref=streams.at[c, 2 + axis, pl.ds(first, count)],
            send_sem=fwd_send.at[axis],
            recv_sem=fwd_recv.at[axis, c if sem is None else sem],
            device_id=(x3, y3)[axis],
            device_id_type=MESH,
        )

    last = [(CHUNKS - 1, 0, CR // 2, CHUNKS - 1), (CHUNKS - 1, CR // 2, CR // 2, CHUNKS)]

    def to_core(h):
        rows = pl.ds(R * h, R)
        return pltpu.make_async_remote_copy(
            src_ref=z.at[rows], dst_ref=core_z.at[rows], send_sem=core_send, recv_sem=core_recv.at[h],
            device_id=core, device_id_type=MESH,
        )

    def whole(ref, send, recv):
        return pltpu.make_async_remote_copy(
            src_ref=ref, dst_ref=ref, send_sem=send, recv_sem=recv, device_id=core, device_id_type=MESH
        )

    def send_ids(p):
        return pltpu.make_async_remote_copy(
            src_ref=ids, dst_ref=r_ids.at[p], send_sem=ids_send, recv_sem=ids_recv.at[p],
            device_id=partners[p], device_id_type=MESH,
        )

    def forward_ids(axis):
        return pltpu.make_async_remote_copy(
            src_ref=r_ids.at[axis], dst_ref=r_ids.at[2 + axis], send_sem=ids_send, recv_sem=ids_recv.at[2 + axis],
            device_id=(x3, y3)[axis], device_id_type=MESH,
        )

    def send_inv(p):
        return pltpu.make_async_remote_copy(
            src_ref=inv_row, dst_ref=r_inv.at[p], send_sem=den_send, recv_sem=den_recv.at[p // 4],
            device_id=partners[p], device_id_type=MESH,
        )

    def normalise(first, count):
        rows = pl.ds(first, count)
        x = raw[rows]
        ir = lax.rsqrt(jnp.sum(x * x, axis=1, keepdims=True) + 1e-06)
        inv_r[rows] = ir
        z[rows] = x * ir

    def launch(*piece):
        direct(0, *piece).start()
        direct(1, *piece).start()

    loads[0].wait()
    normalise(0, CR)
    loads[2].wait()
    for q in range(4):
        ids[pl.ds(2 * q, 2)] = ids_int[...].astype(F32)
    pl.semaphore_wait(barrier, 5)
    launch(0)
    for p in (0, 1, 4):
        send_ids(p).start()
    normalise(CR, R - CR)
    launch(1)
    to_core(0).start()
    for c in range(2, CHUNKS // 2):
        launch(c)
    loads[1].wait()
    normalise(R, R)
    launch(CHUNKS // 2)
    to_core(1).start()
    for c in range(CHUNKS // 2 + 1, CHUNKS - 1):
        launch(c)
    for piece in last:
        launch(*piece)

    hi, lo = split(z[...] * LOGIT)
    zl_hi[...] = hi
    zl_lo[...] = lo
    d = jnp.exp2(LOGIT * jnp.sum(z[pl.ds(0, R)] * z[pl.ds(R, R)], axis=1, keepdims=True))
    diag[...] = d
    lane = lax.broadcasted_iota(jnp.int32, (R, 128), 1)
    start = jnp.where(lane == 0, d, 0.0)
    den_acc[pl.ds(0, R)] = start
    den_acc[pl.ds(R, R)] = start
    for q in range(2):
        id_col[pl.ds(128 * q, 128)] = jnp.broadcast_to(ids[pl.ds(q, 1)], (128, 128)).T

    def scores(lane, keys, key_ids):
        width = keys.shape[0]
        place = pl.ds(lane, width)
        khi, klo = split(keys)
        k_hi[place] = khi
        k_lo[place] = klo
        keep = jnp.concatenate([id_col[...]] * (width // 128), axis=1) != key_ids
        s = dot_t(zl_hi[...], khi) + dot_t(zl_hi[...], klo) + dot_t(zl_lo[...], khi)
        e = jnp.where(jnp.concatenate([keep, keep], axis=0), jnp.exp2(s), 0.0)
        den_acc[...] += sum(e[:, q : q + 128] for q in range(0, width, 128))
        ehi, elo = split(e)
        e_hi[:, place] = ehi
        e_lo[:, place] = elo

    def gather(group):
        place = pl.ds(1024 * group, 1024)
        part = dot(e_hi[:, place], k_hi[place]) + dot(e_hi[:, place], k_lo[place]) + dot(e_lo[:, place], k_hi[place])
        acc[...] = part if group == 0 else acc[...] + part

    def pair_ids(ref):
        return jnp.concatenate([ref[pl.ds(0, 1)], ref[pl.ds(1, 1)]], axis=1)

    def pass_on(*piece):
        for axis in range(2):
            direct(axis, *piece).wait_recv()
            forward(axis, *piece).start()

    own_ids = pair_ids(ids)
    scores(0, z[pl.ds(0, R)], own_ids)
    scores(R, z[pl.ds(R, R)], own_ids)
    pass_on(0)
    for axis in range(2):
        send_ids(axis).wait_recv()
        forward_ids(axis).start()
    send_ids(4).wait_recv()
    core_ids = pair_ids(r_ids.at[4])
    pass_on(1)
    to_core(0).wait_recv()
    scores(2 * R, core_z[pl.ds(0, R)], core_ids)
    pass_on(2)
    to_core(1).wait_recv()
    scores(3 * R, core_z[pl.ds(R, R)], core_ids)
    pass_on(3)
    gather(0)
    for axis in range(2):
        forward_ids(axis).wait_recv()

    left = lax.broadcasted_iota(jnp.int32, (8, 128), 1) < 64

    def mixed(refs):
        a, b, c, d = (refs[p] for p in range(4))
        turn = lambda x: pltpu.roll(x, 64, 1)
        first = jnp.concatenate([jnp.where(left, a, turn(b)), jnp.where(left, c, turn(d))], axis=1)
        second = jnp.concatenate([jnp.where(left, turn(a), b), jnp.where(left, turn(c), d)], axis=1)
        return first, second

    first, second = mixed(r_ids)
    for q in range(2):
        id_rows[pl.ds(2 * q, 1)] = first[q : q + 1]
        id_rows[pl.ds(2 * q + 1, 1)] = second[q : q + 1]

    def stream_scores(c):
        for axis in range(2):
            forward(axis, c).wait_recv()
        lane = pl.multiple_of(4 * R + 4 * CR * c, 4 * CR)
        scores(lane, streams[c].reshape(4 * CR, D), id_rows[pl.ds(c % 4, 1)])

    def stream_step(c, carry):
        stream_scores(c)
        pass_on(c + 4)
        return carry

    lax.fori_loop(0, CHUNKS - 5, stream_step, 0)
    stream_scores(CHUNKS - 5)
    pass_on(*last[0])
    pass_on(*last[1])
    end = CHUNKS - 1
    end_lane = 4 * R + 4 * CR * end
    end_ids = id_rows[pl.ds(end % 4, 1)]
    scores(end_lane, streams[end, pl.ds(0, 2)].reshape(2 * CR, D), end_ids[:, :128])
    gather(1)
    for c in range(CHUNKS - 4, end):
        stream_scores(c)

    s_hi = den_acc[...].astype(BF16)
    rest = den_acc[...] - s_hi.astype(F32)
    s_mid, s_lo = split(rest)
    ones = jnp.ones((8, 128), BF16)
    inv_row[...] = jnp.zeros_like(inv_row)
    sums = dot_t(ones, s_hi) + dot_t(ones, s_mid) + dot_t(ones, s_lo)
    end_keep = jnp.concatenate([jnp.broadcast_to(end_ids[:, 128:], (128, 128)).T] * 4, axis=1) != jnp.concatenate(
        [own_ids, own_ids], axis=1
    )

    for piece in last:
        for axis in range(2):
            forward(axis, *piece).wait_recv()
    khi, klo = split(streams[end, pl.ds(2, 2)].reshape(2 * CR, D))
    turned = dot_t(khi, zl_hi[...]) + dot_t(klo, zl_hi[...]) + dot_t(khi, zl_lo[...])
    turned = jnp.where(end_keep, jnp.exp2(turned), 0.0)
    own_inv = 1.0 / (sums[0:1] + jnp.sum(turned, axis=0, keepdims=True))
    for q in range(4):
        inv_row[pl.ds(q, 1)] = own_inv[:, 128 * q : 128 * (q + 1)]
    for p in range(5):
        send_inv(p).start()

    scores(end_lane + 128, streams[end, pl.ds(2, 2)].reshape(2 * CR, D), end_ids[:, 128:])
    gather(2)
    centre = jnp.mean(own_inv, axis=1, keepdims=True)
    inv_col = 1.0 / jnp.sum(den_acc[...], axis=1, keepdims=True)
    coef = diag[...] * (inv_col[:R] + inv_col[R:]) - 1.0 / TAU
    for h in range(2):
        rows, others = pl.ds(R * h, R), pl.ds(R * (1 - h), R)
        acc[rows] = (inv_col[R * h : R * (h + 1)] + centre) * acc[rows] + coef * z[others]

    def spread(slot, row, lane, values):
        inv_rows[0:1, pl.ds(256 * slot + lane, values.shape[1])] = values[row : row + 1] - centre

    def weighted(first, count):
        place = pl.ds(256 * first, 256 * count)
        off = jnp.broadcast_to(inv_rows[0:1, place], (16, 256 * count)).astype(BF16)[None]
        e = e_hi[:, place].reshape(2 * R // 16, 16, 256 * count)
        return dot((e * off).reshape(2 * R, 256 * count), k_hi[place])

    send_inv(4).wait_recv()
    own, other = inv_row[...], r_inv[4]
    for q in range(4):
        spread(q // 2, q, 128 * (q % 2), own)
        spread(2 + q // 2, q, 128 * (q % 2), other)
    acc[...] += weighted(0, 4)

    whole(r_inv.at[pl.ds(0, 4)], den_send, den_recv.at[0]).wait_recv()
    first, second = mixed(r_inv)
    for q in range(4):
        spread(4 + 2 * q, q, 0, first)
        spread(5 + 2 * q, q, 0, second)
    grad[...] = acc[...] + weighted(4, STEPS - 4)

    for axis in range(2):
        whole(z, direct_send.at[axis], core_recv.at[0]).wait_send()
        whole(z, fwd_send.at[axis], core_recv.at[0]).wait_send()
    whole(z, core_send, core_recv.at[0]).wait_send()
    whole(r_ids, ids_send, core_recv.at[0]).wait_send()
    whole(r_inv, den_send, core_recv.at[0]).wait_send()


def finish(z, grad, inv_r, out_one, out_two, result, out_sem):
    outs = []
    for c in range(4):
        rows = pl.ds(128 * c, 128)
        g, own = grad[rows], z[rows]
        result[rows] = (g - own * jnp.sum(own * g, axis=1, keepdims=True)) * inv_r[rows]
        copy = pltpu.make_async_copy(
            result.at[rows], (out_one, out_two)[c // 2].at[pl.ds(128 * (c % 2), 128)], out_sem.at[c]
        )
        copy.start()
        outs.append(copy)
    for copy in outs:
        copy.wait()


def on_device(view_one, view_two, node_ids):
    dma = pltpu.SemaphoreType.DMA
    hbm = pl.BlockSpec(memory_space=pltpu.HBM)
    vmem = pl.BlockSpec(memory_space=pltpu.VMEM)
    middle = pl.pallas_call(
        kernel,
        out_shape=(
            pltpu.VMEM((2 * R, D), F32),
            pltpu.VMEM((2 * R, D), F32),
            pltpu.VMEM((2 * R, 1), F32),
        ),
        in_specs=[hbm] * 3,
        out_specs=(vmem,) * 3,
        scratch_shapes=[
            pltpu.VMEM((2 * R, D), F32),
            pltpu.VMEM((2 * R, D), BF16),
            pltpu.VMEM((2 * R, D), BF16),
            pltpu.VMEM((2 * R, D), F32),
            pltpu.VMEM((CHUNKS, 4, CR, D), F32),
            pltpu.VMEM((256 * STEPS, D), BF16),
            pltpu.VMEM((256 * STEPS, D), BF16),
            pltpu.VMEM((2 * R, 256 * STEPS), BF16),
            pltpu.VMEM((2 * R, 256 * STEPS), BF16),
            pltpu.VMEM((2 * R, D), F32),
            pltpu.VMEM((2 * R, 128), F32),
            pltpu.VMEM((R, 128), F32),
            pltpu.VMEM((2, 128), jnp.int32),
            pltpu.VMEM((8, 128), F32),
            pltpu.VMEM((5, 8, 128), F32),
            pltpu.VMEM((8, 256), F32),
            pltpu.VMEM((8, 128), F32),
            pltpu.VMEM((5, 8, 128), F32),
            pltpu.VMEM((8, 256 * STEPS), F32),
            pltpu.VMEM((R, 1), F32),
            dma((3,)),
            dma((2,)),
            dma((2, CHUNKS + 1)),
            dma((2,)),
            dma((2, CHUNKS + 1)),
            dma,
            dma((2,)),
            dma,
            dma((5,)),
            dma,
            dma((2,)),
        ],
        compiler_params=pltpu.CompilerParams(
            collective_id=0, has_side_effects=True, vmem_limit_bytes=32 * 1024 * 1024
        ),
    )(*(pltpu.with_memory_space_constraint(x, pltpu.HBM) for x in (view_one, view_two, node_ids.reshape(2, 128))))
    return pl.pallas_call(
        finish,
        out_shape=(jax.ShapeDtypeStruct((R, D), F32), jax.ShapeDtypeStruct((R, D), F32)),
        in_specs=[vmem] * 3,
        out_specs=(hbm, hbm),
        scratch_shapes=[pltpu.VMEM((2 * R, D), F32), dma((4,))],
        compiler_params=pltpu.CompilerParams(vmem_limit_bytes=4 * 1024 * 1024),
    )(*middle)


def solution(mesh):
    rows = P(("blk", "grp"), None)
    return jax.shard_map(
        on_device,
        mesh=mesh,
        in_specs=(rows, rows, P(("blk", "grp"))),
        out_specs=(rows, rows),
        check_vma=False,
    )
```

```python
import math

import jax
import jax.numpy as jnp
from jax import lax
from jax.experimental import pallas as pl
from jax.experimental.pallas import tpu as pltpu
from jax.sharding import PartitionSpec as P

MESH = pl.DeviceIdType.MESH
F32, BF16 = jnp.float32, jnp.bfloat16

R = 256
D = 256
CHUNKS = 8
CR = 2 * R // CHUNKS
TAU = 0.5
LOGIT = 1.0 / (TAU * math.log(2.0))
STEPS = 12


def flip(n, bit):
    return n + bit - 2 * bit * ((n // bit) % 2)


def split(x):
    hi = x.astype(BF16)
    return hi, (x - hi.astype(F32)).astype(BF16)


def dot_t(a, b):
    return lax.dot_general(a, b, (((1,), (1,)), ((), ())), preferred_element_type=F32)


def dot(a, b):
    return lax.dot_general(a, b, (((1,), (0,)), ((), ())), preferred_element_type=F32)


def kernel(
    one_hbm, two_hbm, ids_hbm, z, acc, inv_r, k_hi, e_hi, inv_rows,
    raw, zl_hi, zl_lo, core_z, streams, k_lo, e_lo, den_acc, id_col, ids_int, ids, r_ids, id_rows,
    inv_row, r_inv, diag,
    load_sem, direct_send, direct_recv, fwd_send, fwd_recv, core_send, core_recv, ids_send, ids_recv, den_send, den_recv,
):
    blk, grp = lax.axis_index("blk"), lax.axis_index("grp")
    core = (flip(blk, 1), grp)
    side = blk % 2

    def turn(x, y):
        return tuple(p + side * (q - p) for p, q in zip(x, y)), tuple(q + side * (p - q) for p, q in zip(x, y))

    x1, y1 = turn((flip(blk, 2), grp), (blk, flip(grp, 2)))
    x3, y3 = turn((flip(blk, 2), flip(grp, 1)), (blk, flip(flip(grp, 2), 4)))
    x2, y2 = turn((blk, flip(grp, 1)), (blk, flip(grp, 4)))
    partners = (x1, y1, x2, y2, core)

    barrier = pltpu.get_barrier_semaphore()
    for peer in (x1, x3, y1, y3, core):
        pl.semaphore_signal(barrier, inc=1, device_id=peer, device_id_type=MESH)

    loads = [
        pltpu.make_async_copy(one_hbm, raw.at[pl.ds(0, R)], load_sem.at[0]),
        pltpu.make_async_copy(two_hbm, raw.at[pl.ds(R, R)], load_sem.at[1]),
        pltpu.make_async_copy(ids_hbm, ids_int, load_sem.at[2]),
    ]
    for copy in loads:
        copy.start()

    def direct(axis, c, first=0, count=CR, sem=None):
        return pltpu.make_async_remote_copy(
            src_ref=z.at[pl.ds(CR * c + first, count)],
            dst_ref=streams.at[c, axis, pl.ds(first, count)],
            send_sem=direct_send.at[axis],
            recv_sem=direct_recv.at[axis, c if sem is None else sem],
            device_id=(x1, y1)[axis],
            device_id_type=MESH,
        )

    def forward(axis, c, first=0, count=CR, sem=None):
        return pltpu.make_async_remote_copy(
            src_ref=streams.at[c, axis, pl.ds(first, count)],
            dst_ref=streams.at[c, 2 + axis, pl.ds(first, count)],
            send_sem=fwd_send.at[axis],
            recv_sem=fwd_recv.at[axis, c if sem is None else sem],
            device_id=(x3, y3)[axis],
            device_id_type=MESH,
        )

    opening = [(0, 0, CR // 2, CHUNKS + 1), (0, CR // 2, CR // 2, 0)]
    last = [(CHUNKS - 1, 0, CR // 2, CHUNKS - 1), (CHUNKS - 1, CR // 2, CR // 2, CHUNKS)]

    def to_core(h):
        rows = pl.ds(R * h, R)
        return pltpu.make_async_remote_copy(
            src_ref=z.at[rows], dst_ref=core_z.at[rows], send_sem=core_send, recv_sem=core_recv.at[h],
            device_id=core, device_id_type=MESH,
        )

    def whole(ref, send, recv):
        return pltpu.make_async_remote_copy(
            src_ref=ref, dst_ref=ref, send_sem=send, recv_sem=recv, device_id=core, device_id_type=MESH
        )

    def send_ids(p):
        return pltpu.make_async_remote_copy(
            src_ref=ids, dst_ref=r_ids.at[p], send_sem=ids_send, recv_sem=ids_recv.at[p],
            device_id=partners[p], device_id_type=MESH,
        )

    def forward_ids(axis):
        return pltpu.make_async_remote_copy(
            src_ref=r_ids.at[axis], dst_ref=r_ids.at[2 + axis], send_sem=ids_send, recv_sem=ids_recv.at[2 + axis],
            device_id=(x3, y3)[axis], device_id_type=MESH,
        )

    def send_inv(p):
        return pltpu.make_async_remote_copy(
            src_ref=inv_row, dst_ref=r_inv.at[p], send_sem=den_send, recv_sem=den_recv.at[p // 4],
            device_id=partners[p], device_id_type=MESH,
        )

    def normalise(first, count):
        rows = pl.ds(first, count)
        x = raw[rows]
        ir = lax.rsqrt(jnp.sum(x * x, axis=1, keepdims=True) + 1e-06)
        inv_r[rows] = ir
        z[rows] = x * ir

    def launch(*piece):
        direct(0, *piece).start()
        direct(1, *piece).start()

    loads[0].wait()
    normalise(0, CR)
    loads[2].wait()
    for q in range(4):
        ids[pl.ds(2 * q, 2)] = ids_int[...].astype(F32)
    pl.semaphore_wait(barrier, 5)
    for piece in opening:
        launch(*piece)
    for p in (0, 1, 4):
        send_ids(p).start()
    normalise(CR, R - CR)
    launch(1)
    to_core(0).start()
    for c in range(2, CHUNKS // 2):
        launch(c)
    loads[1].wait()
    normalise(R, R)
    launch(CHUNKS // 2)
    to_core(1).start()
    for c in range(CHUNKS // 2 + 1, CHUNKS - 1):
        launch(c)
    for piece in last:
        launch(*piece)

    hi, lo = split(z[...] * LOGIT)
    zl_hi[...] = hi
    zl_lo[...] = lo
    d = jnp.exp2(LOGIT * jnp.sum(z[pl.ds(0, R)] * z[pl.ds(R, R)], axis=1, keepdims=True))
    diag[...] = d
    lane = lax.broadcasted_iota(jnp.int32, (R, 128), 1)
    start = jnp.where(lane == 0, d, 0.0)
    den_acc[pl.ds(0, R)] = start
    den_acc[pl.ds(R, R)] = start
    for q in range(2):
        id_col[pl.ds(128 * q, 128)] = jnp.broadcast_to(ids[pl.ds(q, 1)], (128, 128)).T

    def scores(lane, keys, key_ids):
        width = keys.shape[0]
        place = pl.ds(lane, width)
        khi, klo = split(keys)
        k_hi[place] = khi
        k_lo[place] = klo
        keep = jnp.concatenate([id_col[...]] * (width // 128), axis=1) != key_ids
        s = dot_t(zl_hi[...], khi) + dot_t(zl_hi[...], klo) + dot_t(zl_lo[...], khi)
        e = jnp.where(jnp.concatenate([keep, keep], axis=0), jnp.exp2(s), 0.0)
        den_acc[...] += sum(e[:, q : q + 128] for q in range(0, width, 128))
        ehi, elo = split(e)
        e_hi[:, place] = ehi
        e_lo[:, place] = elo

    def gather(group):
        place = pl.ds(1024 * group, 1024)
        part = dot(e_hi[:, place], k_hi[place]) + dot(e_hi[:, place], k_lo[place]) + dot(e_lo[:, place], k_hi[place])
        acc[...] = part if group == 0 else acc[...] + part

    def pair_ids(ref):
        return jnp.concatenate([ref[pl.ds(0, 1)], ref[pl.ds(1, 1)]], axis=1)

    def pass_on(*piece):
        for axis in range(2):
            direct(axis, *piece).wait_recv()
            forward(axis, *piece).start()

    own_ids = pair_ids(ids)
    scores(0, z[pl.ds(0, R)], own_ids)
    scores(R, z[pl.ds(R, R)], own_ids)
    for piece in opening:
        pass_on(*piece)
    for axis in range(2):
        send_ids(axis).wait_recv()
        forward_ids(axis).start()
    send_ids(4).wait_recv()
    core_ids = pair_ids(r_ids.at[4])
    pass_on(1)
    to_core(0).wait_recv()
    scores(2 * R, core_z[pl.ds(0, R)], core_ids)
    pass_on(2)
    to_core(1).wait_recv()
    scores(3 * R, core_z[pl.ds(R, R)], core_ids)
    pass_on(3)
    gather(0)
    for axis in range(2):
        forward_ids(axis).wait_recv()

    left = lax.broadcasted_iota(jnp.int32, (8, 128), 1) < 64

    def mixed(refs):
        a, b, c, d = (refs[p] for p in range(4))
        turn = lambda x: pltpu.roll(x, 64, 1)
        first = jnp.concatenate([jnp.where(left, a, turn(b)), jnp.where(left, c, turn(d))], axis=1)
        second = jnp.concatenate([jnp.where(left, turn(a), b), jnp.where(left, turn(c), d)], axis=1)
        return first, second

    first, second = mixed(r_ids)
    for q in range(2):
        id_rows[pl.ds(2 * q, 1)] = first[q : q + 1]
        id_rows[pl.ds(2 * q + 1, 1)] = second[q : q + 1]

    def stream_scores(c, pieces=None):
        for piece in pieces or [(c,)]:
            for axis in range(2):
                forward(axis, *piece).wait_recv()
        lane = pl.multiple_of(4 * R + 4 * CR * c, 4 * CR)
        scores(lane, streams[c].reshape(4 * CR, D), id_rows[pl.ds(c % 4, 1)])

    def stream_step(c, carry):
        stream_scores(c)
        pass_on(c + 4)
        return carry

    stream_scores(0, opening)
    pass_on(4)
    lax.fori_loop(1, CHUNKS - 5, stream_step, 0)
    stream_scores(CHUNKS - 5)
    pass_on(*last[0])
    pass_on(*last[1])
    end = CHUNKS - 1
    end_lane = 4 * R + 4 * CR * end
    end_ids = id_rows[pl.ds(end % 4, 1)]
    scores(end_lane, streams[end, pl.ds(0, 2)].reshape(2 * CR, D), end_ids[:, :128])
    gather(1)
    for c in range(CHUNKS - 4, end):
        stream_scores(c)

    s_hi = den_acc[...].astype(BF16)
    rest = den_acc[...] - s_hi.astype(F32)
    s_mid, s_lo = split(rest)
    ones = jnp.ones((8, 128), BF16)
    inv_row[...] = jnp.zeros_like(inv_row)
    sums = dot_t(ones, s_hi) + dot_t(ones, s_mid) + dot_t(ones, s_lo)
    end_keep = jnp.concatenate([jnp.broadcast_to(end_ids[:, 128:], (128, 128)).T] * 4, axis=1) != jnp.concatenate(
        [own_ids, own_ids], axis=1
    )

    for piece in last:
        for axis in range(2):
            forward(axis, *piece).wait_recv()
    khi, klo = split(streams[end, pl.ds(2, 2)].reshape(2 * CR, D))
    turned = dot_t(khi, zl_hi[...]) + dot_t(klo, zl_hi[...]) + dot_t(khi, zl_lo[...])
    turned = jnp.where(end_keep, jnp.exp2(turned), 0.0)
    own_inv = 1.0 / (sums[0:1] + jnp.sum(turned, axis=0, keepdims=True))
    for q in range(4):
        inv_row[pl.ds(q, 1)] = own_inv[:, 128 * q : 128 * (q + 1)]
    for p in range(5):
        send_inv(p).start()

    scores(end_lane + 128, streams[end, pl.ds(2, 2)].reshape(2 * CR, D), end_ids[:, 128:])
    gather(2)
    centre = jnp.mean(own_inv, axis=1, keepdims=True)
    inv_col = 1.0 / jnp.sum(den_acc[...], axis=1, keepdims=True)
    coef = diag[...] * (inv_col[:R] + inv_col[R:]) - 1.0 / TAU
    for h in range(2):
        rows, others = pl.ds(R * h, R), pl.ds(R * (1 - h), R)
        acc[rows] = (inv_col[R * h : R * (h + 1)] + centre) * acc[rows] + coef * z[others]

    def spread(slot, row, lane, values):
        inv_rows[0:1, pl.ds(256 * slot + lane, values.shape[1])] = values[row : row + 1] - centre

    send_inv(4).wait_recv()
    own, other = inv_row[...], r_inv[4]
    for q in range(4):
        spread(q // 2, q, 128 * (q % 2), own)
        spread(2 + q // 2, q, 128 * (q % 2), other)
    acc[...] += weighted(e_hi, k_hi, inv_rows, pl.ds(0, 2 * R), pl.ds(0, 4 * R))

    whole(r_inv.at[pl.ds(0, 4)], den_send, den_recv.at[0]).wait_recv()
    first, second = mixed(r_inv)
    for q in range(4):
        spread(4 + 2 * q, q, 0, first)
        spread(5 + 2 * q, q, 0, second)

    for axis in range(2):
        whole(z, direct_send.at[axis], core_recv.at[0]).wait_send()
        whole(z, fwd_send.at[axis], core_recv.at[0]).wait_send()
    whole(z, core_send, core_recv.at[0]).wait_send()
    whole(r_ids, ids_send, core_recv.at[0]).wait_send()
    whole(r_inv, den_send, core_recv.at[0]).wait_send()


def weighted(e_hi, k_hi, inv_rows, rows, keys):
    off = jnp.broadcast_to(inv_rows[0:1, keys], (16, keys.size)).astype(BF16)[None]
    e = e_hi[rows, keys].reshape(rows.size // 16, 16, keys.size)
    return dot((e * off).reshape(rows.size, keys.size), k_hi[keys])


def finish(z, acc, inv_r, k_hi, e_hi, inv_rows, out_one, out_two, result, out_sem):
    outs = []
    for h in range(2):
        rows = pl.ds(R * h, R)
        g = acc[rows] + weighted(e_hi, k_hi, inv_rows, rows, pl.ds(4 * R, (STEPS - 4) * 256))
        own = z[rows]
        result[rows] = (g - own * jnp.sum(own * g, axis=1, keepdims=True)) * inv_r[rows]
        copy = pltpu.make_async_copy(result.at[rows], (out_one, out_two)[h], out_sem.at[h])
        copy.start()
        outs.append(copy)
    for copy in outs:
        copy.wait()


def on_device(view_one, view_two, node_ids):
    dma = pltpu.SemaphoreType.DMA
    hbm = pl.BlockSpec(memory_space=pltpu.HBM)
    vmem = pl.BlockSpec(memory_space=pltpu.VMEM)
    middle = pl.pallas_call(
        kernel,
        out_shape=(
            pltpu.VMEM((2 * R, D), F32),
            pltpu.VMEM((2 * R, D), F32),
            pltpu.VMEM((2 * R, 1), F32),
            pltpu.VMEM((256 * STEPS, D), BF16),
            pltpu.VMEM((2 * R, 256 * STEPS), BF16),
            pltpu.VMEM((8, 256 * STEPS), F32),
        ),
        in_specs=[hbm] * 3,
        out_specs=(vmem,) * 6,
        scratch_shapes=[
            pltpu.VMEM((2 * R, D), F32),
            pltpu.VMEM((2 * R, D), BF16),
            pltpu.VMEM((2 * R, D), BF16),
            pltpu.VMEM((2 * R, D), F32),
            pltpu.VMEM((CHUNKS, 4, CR, D), F32),
            pltpu.VMEM((256 * STEPS, D), BF16),
            pltpu.VMEM((2 * R, 256 * STEPS), BF16),
            pltpu.VMEM((2 * R, 128), F32),
            pltpu.VMEM((R, 128), F32),
            pltpu.VMEM((2, 128), jnp.int32),
            pltpu.VMEM((8, 128), F32),
            pltpu.VMEM((5, 8, 128), F32),
            pltpu.VMEM((8, 256), F32),
            pltpu.VMEM((8, 128), F32),
            pltpu.VMEM((5, 8, 128), F32),
            pltpu.VMEM((R, 1), F32),
            dma((3,)),
            dma((2,)),
            dma((2, CHUNKS + 2)),
            dma((2,)),
            dma((2, CHUNKS + 2)),
            dma,
            dma((2,)),
            dma,
            dma((5,)),
            dma,
            dma((2,)),
        ],
        compiler_params=pltpu.CompilerParams(
            collective_id=0, has_side_effects=True, vmem_limit_bytes=32 * 1024 * 1024
        ),
    )(*(pltpu.with_memory_space_constraint(x, pltpu.HBM) for x in (view_one, view_two, node_ids.reshape(2, 128))))
    return pl.pallas_call(
        finish,
        out_shape=(jax.ShapeDtypeStruct((R, D), F32), jax.ShapeDtypeStruct((R, D), F32)),
        in_specs=[vmem] * 6,
        out_specs=(hbm, hbm),
        scratch_shapes=[pltpu.VMEM((2 * R, D), F32), dma((2,))],
        compiler_params=pltpu.CompilerParams(vmem_limit_bytes=8 * 1024 * 1024),
    )(*middle)


def solution(mesh):
    rows = P(("blk", "grp"), None)
    return jax.shard_map(
        on_device,
        mesh=mesh,
        in_specs=(rows, rows, P(("blk", "grp"))),
        out_specs=(rows, rows),
        check_vma=False,
    )
```

```python
import math

import jax
import jax.numpy as jnp
from jax import lax
from jax.experimental import pallas as pl
from jax.experimental.pallas import tpu as pltpu
from jax.sharding import PartitionSpec as P

MESH = pl.DeviceIdType.MESH
F32, BF16 = jnp.float32, jnp.bfloat16

R = 256
D = 256
CHUNKS = 8
CR = 2 * R // CHUNKS
TAU = 0.5
LOGIT = 1.0 / (TAU * math.log(2.0))
STEPS = 12


def flip(n, bit):
    return n + bit - 2 * bit * ((n // bit) % 2)


def split(x):
    hi = x.astype(BF16)
    return hi, (x - hi.astype(F32)).astype(BF16)


def dot_t(a, b):
    return lax.dot_general(a, b, (((1,), (1,)), ((), ())), preferred_element_type=F32)


def dot(a, b):
    return lax.dot_general(a, b, (((1,), (0,)), ((), ())), preferred_element_type=F32)


def kernel(
    one_hbm, two_hbm, ids_hbm, z, acc, inv_r, k_hi, e_hi, inv_rows,
    raw, zl_hi, zl_lo, core_z, streams, k_lo, e_lo, den_acc, id_col, ids_int, ids, r_ids, id_rows,
    inv_row, r_inv, diag,
    load_sem, direct_send, direct_recv, fwd_send, fwd_recv, core_send, core_recv, ids_send, ids_recv, den_send, den_recv,
):
    blk, grp = lax.axis_index("blk"), lax.axis_index("grp")
    core = (flip(blk, 1), grp)
    side = blk % 2

    def turn(x, y):
        return tuple(p + side * (q - p) for p, q in zip(x, y)), tuple(q + side * (p - q) for p, q in zip(x, y))

    x1, y1 = turn((flip(blk, 2), grp), (blk, flip(grp, 2)))
    x3, y3 = turn((flip(blk, 2), flip(grp, 1)), (blk, flip(flip(grp, 2), 4)))
    x2, y2 = turn((blk, flip(grp, 1)), (blk, flip(grp, 4)))
    partners = (x1, y1, x2, y2, core)

    barrier = pltpu.get_barrier_semaphore()
    for peer in (x1, x3, y1, y3, core):
        pl.semaphore_signal(barrier, inc=1, device_id=peer, device_id_type=MESH)

    loads = [
        pltpu.make_async_copy(one_hbm, raw.at[pl.ds(0, R)], load_sem.at[0]),
        pltpu.make_async_copy(two_hbm, raw.at[pl.ds(R, R)], load_sem.at[1]),
        pltpu.make_async_copy(ids_hbm, ids_int, load_sem.at[2]),
    ]
    for copy in loads:
        copy.start()

    def direct(axis, c, first=0, count=CR, sem=None):
        source = raw.at[pl.ds(CR * c + first, count)]
        if isinstance(c, int):
            view, at = (one_hbm, two_hbm)[c // (CHUNKS // 2)], CR * (c % (CHUNKS // 2))
            source = view.at[pl.ds(at + first, count)]
        return pltpu.make_async_remote_copy(
            src_ref=source,
            dst_ref=streams.at[c, axis, pl.ds(first, count)],
            send_sem=direct_send.at[axis],
            recv_sem=direct_recv.at[axis, c if sem is None else sem],
            device_id=(x1, y1)[axis],
            device_id_type=MESH,
        )

    def forward(axis, c, first=0, count=CR, sem=None):
        return pltpu.make_async_remote_copy(
            src_ref=streams.at[c, axis, pl.ds(first, count)],
            dst_ref=streams.at[c, 2 + axis, pl.ds(first, count)],
            send_sem=fwd_send.at[axis],
            recv_sem=fwd_recv.at[axis, c if sem is None else sem],
            device_id=(x3, y3)[axis],
            device_id_type=MESH,
        )

    opening = [(0, 0, CR // 2, CHUNKS + 1), (0, CR // 2, CR // 2, 0)]
    last = [(CHUNKS - 1, 0, CR // 2, CHUNKS - 1), (CHUNKS - 1, CR // 2, CR // 2, CHUNKS)]

    def to_core(h):
        rows = pl.ds(R * h, R)
        return pltpu.make_async_remote_copy(
            src_ref=(one_hbm, two_hbm)[h], dst_ref=core_z.at[rows], send_sem=core_send, recv_sem=core_recv.at[h],
            device_id=core, device_id_type=MESH,
        )

    def whole(ref, send, recv):
        return pltpu.make_async_remote_copy(
            src_ref=ref, dst_ref=ref, send_sem=send, recv_sem=recv, device_id=core, device_id_type=MESH
        )

    def send_ids(p):
        return pltpu.make_async_remote_copy(
            src_ref=ids, dst_ref=r_ids.at[p], send_sem=ids_send, recv_sem=ids_recv.at[p],
            device_id=partners[p], device_id_type=MESH,
        )

    def forward_ids(axis):
        return pltpu.make_async_remote_copy(
            src_ref=r_ids.at[axis], dst_ref=r_ids.at[2 + axis], send_sem=ids_send, recv_sem=ids_recv.at[2 + axis],
            device_id=(x3, y3)[axis], device_id_type=MESH,
        )

    def send_inv(p):
        return pltpu.make_async_remote_copy(
            src_ref=inv_row, dst_ref=r_inv.at[p], send_sem=den_send, recv_sem=den_recv.at[p // 4],
            device_id=partners[p], device_id_type=MESH,
        )

    def inverse_radius(x):
        return lax.rsqrt(jnp.sum(x * x, axis=1, keepdims=True) + 1e-06)

    def unit(x):
        return x * inverse_radius(x)

    def launch(*piece):
        direct(0, *piece).start()
        direct(1, *piece).start()

    pl.semaphore_wait(barrier, 5)
    for piece in opening:
        launch(*piece)
    launch(1)
    for h in range(2):
        to_core(h).start()
    loads[2].wait()
    for q in range(4):
        ids[pl.ds(2 * q, 2)] = ids_int[...].astype(F32)
    for p in (0, 1, 4):
        send_ids(p).start()
    for c in range(2, CHUNKS - 1):
        launch(c)
    for piece in last:
        launch(*piece)
    for h in range(2):
        rows = pl.ds(R * h, R)
        loads[h].wait()
        x = raw[rows]
        ir = inverse_radius(x)
        inv_r[rows] = ir
        z[rows] = x * ir

    hi, lo = split(z[...] * LOGIT)
    zl_hi[...] = hi
    zl_lo[...] = lo
    d = jnp.exp2(LOGIT * jnp.sum(z[pl.ds(0, R)] * z[pl.ds(R, R)], axis=1, keepdims=True))
    diag[...] = d
    lane = lax.broadcasted_iota(jnp.int32, (R, 128), 1)
    start = jnp.where(lane == 0, d, 0.0)
    den_acc[pl.ds(0, R)] = start
    den_acc[pl.ds(R, R)] = start
    for q in range(2):
        id_col[pl.ds(128 * q, 128)] = jnp.broadcast_to(ids[pl.ds(q, 1)], (128, 128)).T

    def scores(lane, keys, key_ids):
        width = keys.shape[0]
        place = pl.ds(lane, width)
        khi, klo = split(keys)
        k_hi[place] = khi
        k_lo[place] = klo
        keep = jnp.concatenate([id_col[...]] * (width // 128), axis=1) != key_ids
        s = dot_t(zl_hi[...], khi) + dot_t(zl_hi[...], klo) + dot_t(zl_lo[...], khi)
        e = jnp.where(jnp.concatenate([keep, keep], axis=0), jnp.exp2(s), 0.0)
        den_acc[...] += sum(e[:, q : q + 128] for q in range(0, width, 128))
        ehi, elo = split(e)
        e_hi[:, place] = ehi
        e_lo[:, place] = elo

    def gather(group):
        place = pl.ds(1024 * group, 1024)
        part = dot(e_hi[:, place], k_hi[place]) + dot(e_hi[:, place], k_lo[place]) + dot(e_lo[:, place], k_hi[place])
        acc[...] = part if group == 0 else acc[...] + part

    def pair_ids(ref):
        return jnp.concatenate([ref[pl.ds(0, 1)], ref[pl.ds(1, 1)]], axis=1)

    def pass_on(*piece):
        for axis in range(2):
            direct(axis, *piece).wait_recv()
            forward(axis, *piece).start()

    own_ids = pair_ids(ids)
    scores(0, z[pl.ds(0, R)], own_ids)
    scores(R, z[pl.ds(R, R)], own_ids)
    for piece in opening:
        pass_on(*piece)
    for axis in range(2):
        send_ids(axis).wait_recv()
        forward_ids(axis).start()
    send_ids(4).wait_recv()
    core_ids = pair_ids(r_ids.at[4])
    pass_on(1)
    to_core(0).wait_recv()
    scores(2 * R, unit(core_z[pl.ds(0, R)]), core_ids)
    pass_on(2)
    to_core(1).wait_recv()
    scores(3 * R, unit(core_z[pl.ds(R, R)]), core_ids)
    pass_on(3)
    gather(0)
    for axis in range(2):
        forward_ids(axis).wait_recv()

    left = lax.broadcasted_iota(jnp.int32, (8, 128), 1) < 64

    def mixed(refs):
        a, b, c, d = (refs[p] for p in range(4))
        turn = lambda x: pltpu.roll(x, 64, 1)
        first = jnp.concatenate([jnp.where(left, a, turn(b)), jnp.where(left, c, turn(d))], axis=1)
        second = jnp.concatenate([jnp.where(left, turn(a), b), jnp.where(left, turn(c), d)], axis=1)
        return first, second

    first, second = mixed(r_ids)
    for q in range(2):
        id_rows[pl.ds(2 * q, 1)] = first[q : q + 1]
        id_rows[pl.ds(2 * q + 1, 1)] = second[q : q + 1]

    def stream_scores(c, pieces=None):
        for piece in pieces or [(c,)]:
            for axis in range(2):
                forward(axis, *piece).wait_recv()
        lane = pl.multiple_of(4 * R + 4 * CR * c, 4 * CR)
        scores(lane, unit(streams[c].reshape(4 * CR, D)), id_rows[pl.ds(c % 4, 1)])

    def stream_step(c, carry):
        stream_scores(c)
        pass_on(c + 4)
        return carry

    stream_scores(0, opening)
    pass_on(4)
    lax.fori_loop(1, CHUNKS - 5, stream_step, 0)
    stream_scores(CHUNKS - 5)
    pass_on(*last[0])
    pass_on(*last[1])
    end = CHUNKS - 1
    end_lane = 4 * R + 4 * CR * end
    end_ids = id_rows[pl.ds(end % 4, 1)]
    scores(end_lane, unit(streams[end, pl.ds(0, 2)].reshape(2 * CR, D)), end_ids[:, :128])
    gather(1)
    for c in range(CHUNKS - 4, end):
        stream_scores(c)

    s_hi = den_acc[...].astype(BF16)
    rest = den_acc[...] - s_hi.astype(F32)
    s_mid, s_lo = split(rest)
    ones = jnp.ones((8, 128), BF16)
    inv_row[...] = jnp.zeros_like(inv_row)
    sums = dot_t(ones, s_hi) + dot_t(ones, s_mid) + dot_t(ones, s_lo)
    end_keep = jnp.concatenate([jnp.broadcast_to(end_ids[:, 128:], (128, 128)).T] * 4, axis=1) != jnp.concatenate(
        [own_ids, own_ids], axis=1
    )

    for piece in last:
        for axis in range(2):
            forward(axis, *piece).wait_recv()
    end_keys = unit(streams[end, pl.ds(2, 2)].reshape(2 * CR, D))
    khi, klo = split(end_keys)
    turned = dot_t(khi, zl_hi[...]) + dot_t(klo, zl_hi[...]) + dot_t(khi, zl_lo[...])
    turned = jnp.where(end_keep, jnp.exp2(turned), 0.0)
    own_inv = 1.0 / (sums[0:1] + jnp.sum(turned, axis=0, keepdims=True))
    for q in range(4):
        inv_row[pl.ds(q, 1)] = own_inv[:, 128 * q : 128 * (q + 1)]
    for p in (2, 3, 0, 1, 4):
        send_inv(p).start()

    scores(end_lane + 128, end_keys, end_ids[:, 128:])
    gather(2)
    centre = jnp.mean(own_inv, axis=1, keepdims=True)
    inv_col = 1.0 / jnp.sum(den_acc[...], axis=1, keepdims=True)
    coef = diag[...] * (inv_col[:R] + inv_col[R:]) - 1.0 / TAU
    for h in range(2):
        rows, others = pl.ds(R * h, R), pl.ds(R * (1 - h), R)
        acc[rows] = (inv_col[R * h : R * (h + 1)] + centre) * acc[rows] + coef * z[others]

    def spread(slot, row, lane, values):
        inv_rows[0:1, pl.ds(256 * slot + lane, values.shape[1])] = values[row : row + 1] - centre

    send_inv(4).wait_recv()
    own, other = inv_row[...], r_inv[4]
    for q in range(4):
        spread(q // 2, q, 128 * (q % 2), own)
        spread(2 + q // 2, q, 128 * (q % 2), other)
    acc[...] += weighted(e_hi, k_hi, inv_rows, pl.ds(0, 2 * R), pl.ds(0, 4 * R))

    whole(r_inv.at[pl.ds(0, 4)], den_send, den_recv.at[0]).wait_recv()
    first, second = mixed(r_inv)
    for q in range(4):
        spread(4 + 2 * q, q, 0, first)
        spread(5 + 2 * q, q, 0, second)

    for axis in range(2):
        whole(z, direct_send.at[axis], core_recv.at[0]).wait_send()
        whole(z, fwd_send.at[axis], core_recv.at[0]).wait_send()
    whole(z, core_send, core_recv.at[0]).wait_send()
    whole(r_ids, ids_send, core_recv.at[0]).wait_send()
    whole(r_inv, den_send, core_recv.at[0]).wait_send()


def weighted(e_hi, k_hi, inv_rows, rows, keys):
    off = jnp.broadcast_to(inv_rows[0:1, keys], (16, keys.size)).astype(BF16)[None]
    e = e_hi[rows, keys].reshape(rows.size // 16, 16, keys.size)
    return dot((e * off).reshape(rows.size, keys.size), k_hi[keys])


def finish(z, acc, inv_r, k_hi, e_hi, inv_rows, out_one, out_two, result, out_sem):
    outs = []
    for h in range(2):
        rows = pl.ds(R * h, R)
        g = acc[rows] + weighted(e_hi, k_hi, inv_rows, rows, pl.ds(4 * R, (STEPS - 4) * 256))
        own = z[rows]
        result[rows] = (g - own * jnp.sum(own * g, axis=1, keepdims=True)) * inv_r[rows]
        copy = pltpu.make_async_copy(result.at[rows], (out_one, out_two)[h], out_sem.at[h])
        copy.start()
        outs.append(copy)
    for copy in outs:
        copy.wait()


def on_device(view_one, view_two, node_ids):
    dma = pltpu.SemaphoreType.DMA
    hbm = pl.BlockSpec(memory_space=pltpu.HBM)
    vmem = pl.BlockSpec(memory_space=pltpu.VMEM)
    middle = pl.pallas_call(
        kernel,
        out_shape=(
            pltpu.VMEM((2 * R, D), F32),
            pltpu.VMEM((2 * R, D), F32),
            pltpu.VMEM((2 * R, 1), F32),
            pltpu.VMEM((256 * STEPS, D), BF16),
            pltpu.VMEM((2 * R, 256 * STEPS), BF16),
            pltpu.VMEM((8, 256 * STEPS), F32),
        ),
        in_specs=[hbm] * 3,
        out_specs=(vmem,) * 6,
        scratch_shapes=[
            pltpu.VMEM((2 * R, D), F32),
            pltpu.VMEM((2 * R, D), BF16),
            pltpu.VMEM((2 * R, D), BF16),
            pltpu.VMEM((2 * R, D), F32),
            pltpu.VMEM((CHUNKS, 4, CR, D), F32),
            pltpu.VMEM((256 * STEPS, D), BF16),
            pltpu.VMEM((2 * R, 256 * STEPS), BF16),
            pltpu.VMEM((2 * R, 128), F32),
            pltpu.VMEM((R, 128), F32),
            pltpu.VMEM((2, 128), jnp.int32),
            pltpu.VMEM((8, 128), F32),
            pltpu.VMEM((5, 8, 128), F32),
            pltpu.VMEM((8, 256), F32),
            pltpu.VMEM((8, 128), F32),
            pltpu.VMEM((5, 8, 128), F32),
            pltpu.VMEM((R, 1), F32),
            dma((3,)),
            dma((2,)),
            dma((2, CHUNKS + 2)),
            dma((2,)),
            dma((2, CHUNKS + 2)),
            dma,
            dma((2,)),
            dma,
            dma((5,)),
            dma,
            dma((2,)),
        ],
        compiler_params=pltpu.CompilerParams(
            collective_id=0, has_side_effects=True, vmem_limit_bytes=32 * 1024 * 1024
        ),
    )(*(pltpu.with_memory_space_constraint(x, pltpu.HBM) for x in (view_one, view_two, node_ids.reshape(2, 128))))
    return pl.pallas_call(
        finish,
        out_shape=(jax.ShapeDtypeStruct((R, D), F32), jax.ShapeDtypeStruct((R, D), F32)),
        in_specs=[vmem] * 6,
        out_specs=(hbm, hbm),
        scratch_shapes=[pltpu.VMEM((2 * R, D), F32), dma((2,))],
        compiler_params=pltpu.CompilerParams(vmem_limit_bytes=8 * 1024 * 1024),
    )(*middle)


def solution(mesh):
    rows = P(("blk", "grp"), None)
    return jax.shard_map(
        on_device,
        mesh=mesh,
        in_specs=(rows, rows, P(("blk", "grp"))),
        out_specs=(rows, rows),
        check_vma=False,
    )
```

```python
import math

import jax
import jax.numpy as jnp
from jax import lax
from jax.experimental import pallas as pl
from jax.experimental.pallas import tpu as pltpu
from jax.sharding import PartitionSpec as P

MESH = pl.DeviceIdType.MESH
F32, BF16 = jnp.float32, jnp.bfloat16

R = 256
D = 256
CHUNKS = 8
CR = 2 * R // CHUNKS
TAU = 0.5
LOGIT = 1.0 / (TAU * math.log(2.0))
STEPS = 12


def flip(n, bit):
    return n + bit - 2 * bit * ((n // bit) % 2)


def split(x):
    hi = x.astype(BF16)
    return hi, (x - hi.astype(F32)).astype(BF16)


def dot_t(a, b):
    return lax.dot_general(a, b, (((1,), (1,)), ((), ())), preferred_element_type=F32)


def dot(a, b):
    return lax.dot_general(a, b, (((1,), (0,)), ((), ())), preferred_element_type=F32)


def kernel(
    one_hbm, two_hbm, ids_hbm, z, acc, inv_r, k_hi, e_hi, inv_rows,
    raw, zl_hi, zl_lo, core_z, streams, k_lo, e_lo, den_acc, id_col, ids_int, ids, r_ids, id_rows,
    inv_row, r_inv, diag,
    load_sem, direct_send, direct_recv, fwd_send, fwd_recv, core_send, core_recv, ids_send, ids_recv, den_send, den_recv,
):
    blk, grp = lax.axis_index("blk"), lax.axis_index("grp")
    core = (flip(blk, 1), grp)
    side = blk % 2

    def turn(x, y):
        return tuple(p + side * (q - p) for p, q in zip(x, y)), tuple(q + side * (p - q) for p, q in zip(x, y))

    x1, y1 = turn((flip(blk, 2), grp), (blk, flip(grp, 2)))
    x3, y3 = turn((flip(blk, 2), flip(grp, 1)), (blk, flip(flip(grp, 2), 4)))
    x2, y2 = turn((blk, flip(grp, 1)), (blk, flip(grp, 4)))
    partners = (x1, y1, x2, y2, core)

    barrier = pltpu.get_barrier_semaphore()
    for peer in (x1, x3, y1, y3, core):
        pl.semaphore_signal(barrier, inc=1, device_id=peer, device_id_type=MESH)

    loads = [
        pltpu.make_async_copy(one_hbm, raw.at[pl.ds(0, R)], load_sem.at[0]),
        pltpu.make_async_copy(two_hbm, raw.at[pl.ds(R, R)], load_sem.at[1]),
        pltpu.make_async_copy(ids_hbm, ids_int, load_sem.at[2]),
    ]
    for copy in loads:
        copy.start()

    def direct(axis, c, first=0, count=CR, sem=None):
        return pltpu.make_async_remote_copy(
            src_ref=z.at[pl.ds(CR * c + first, count)],
            dst_ref=streams.at[c, axis, pl.ds(first, count)],
            send_sem=direct_send.at[axis],
            recv_sem=direct_recv.at[axis, c if sem is None else sem],
            device_id=(x1, y1)[axis],
            device_id_type=MESH,
        )

    def forward(axis, c, first=0, count=CR, sem=None):
        return pltpu.make_async_remote_copy(
            src_ref=streams.at[c, axis, pl.ds(first, count)],
            dst_ref=streams.at[c, 2 + axis, pl.ds(first, count)],
            send_sem=fwd_send.at[axis],
            recv_sem=fwd_recv.at[axis, c if sem is None else sem],
            device_id=(x3, y3)[axis],
            device_id_type=MESH,
        )

    opening = [(0, 0, CR // 2, CHUNKS + 1), (0, CR // 2, CR // 2, 0)]
    last = [(CHUNKS - 1, 0, CR // 2, CHUNKS - 1), (CHUNKS - 1, CR // 2, CR // 2, CHUNKS)]

    def to_core(h):
        rows = pl.ds(R * h, R)
        return pltpu.make_async_remote_copy(
            src_ref=z.at[rows], dst_ref=core_z.at[rows], send_sem=core_send, recv_sem=core_recv.at[h],
            device_id=core, device_id_type=MESH,
        )

    def whole(ref, send, recv):
        return pltpu.make_async_remote_copy(
            src_ref=ref, dst_ref=ref, send_sem=send, recv_sem=recv, device_id=core, device_id_type=MESH
        )

    def send_ids(p):
        return pltpu.make_async_remote_copy(
            src_ref=ids, dst_ref=r_ids.at[p], send_sem=ids_send, recv_sem=ids_recv.at[p],
            device_id=partners[p], device_id_type=MESH,
        )

    def forward_ids(axis):
        return pltpu.make_async_remote_copy(
            src_ref=r_ids.at[axis], dst_ref=r_ids.at[2 + axis], send_sem=ids_send, recv_sem=ids_recv.at[2 + axis],
            device_id=(x3, y3)[axis], device_id_type=MESH,
        )

    def send_inv(p):
        return pltpu.make_async_remote_copy(
            src_ref=inv_row, dst_ref=r_inv.at[p], send_sem=den_send, recv_sem=den_recv.at[p // 4],
            device_id=partners[p], device_id_type=MESH,
        )

    def normalise(first, count):
        rows = pl.ds(first, count)
        x = raw[rows]
        ir = lax.rsqrt(jnp.sum(x * x, axis=1, keepdims=True) + 1e-06)
        inv_r[rows] = ir
        z[rows] = x * ir

    def launch(*piece):
        direct(0, *piece).start()
        direct(1, *piece).start()

    loads[0].wait()
    normalise(0, CR)
    loads[2].wait()
    for q in range(4):
        ids[pl.ds(2 * q, 2)] = ids_int[...].astype(F32)
    pl.semaphore_wait(barrier, 5)
    for piece in opening:
        launch(*piece)
    for p in (0, 1, 4):
        send_ids(p).start()
    normalise(CR, R - CR)
    launch(1)
    to_core(0).start()
    for c in range(2, CHUNKS // 2):
        launch(c)
    loads[1].wait()
    normalise(R, R)
    launch(CHUNKS // 2)
    to_core(1).start()
    for c in range(CHUNKS // 2 + 1, CHUNKS - 1):
        launch(c)
    for piece in last:
        launch(*piece)

    hi, lo = split(z[...] * LOGIT)
    zl_hi[...] = hi
    zl_lo[...] = lo
    d = jnp.exp2(LOGIT * jnp.sum(z[pl.ds(0, R)] * z[pl.ds(R, R)], axis=1, keepdims=True))
    diag[...] = d
    lane = lax.broadcasted_iota(jnp.int32, (R, 128), 1)
    start = jnp.where(lane == 0, d, 0.0)
    den_acc[pl.ds(0, R)] = start
    den_acc[pl.ds(R, R)] = start
    for q in range(2):
        id_col[pl.ds(128 * q, 128)] = jnp.broadcast_to(ids[pl.ds(q, 1)], (128, 128)).T

    def scores(lane, keys, key_ids):
        width = keys.shape[0]
        place = pl.ds(lane, width)
        khi, klo = split(keys)
        k_hi[place] = khi
        k_lo[place] = klo
        keep = jnp.concatenate([id_col[...]] * (width // 128), axis=1) != key_ids
        s = dot_t(zl_hi[...], khi) + dot_t(zl_hi[...], klo) + dot_t(zl_lo[...], khi)
        e = jnp.where(jnp.concatenate([keep, keep], axis=0), jnp.exp2(s), 0.0)
        den_acc[...] += sum(e[:, q : q + 128] for q in range(0, width, 128))
        ehi, elo = split(e)
        e_hi[:, place] = ehi
        e_lo[:, place] = elo

    def gather(group):
        place = pl.ds(1024 * group, 1024)
        part = dot(e_hi[:, place], k_hi[place]) + dot(e_hi[:, place], k_lo[place]) + dot(e_lo[:, place], k_hi[place])
        acc[...] = part if group == 0 else acc[...] + part

    def pair_ids(ref):
        return jnp.concatenate([ref[pl.ds(0, 1)], ref[pl.ds(1, 1)]], axis=1)

    def pass_on(*piece):
        for axis in range(2):
            direct(axis, *piece).wait_recv()
            forward(axis, *piece).start()

    own_ids = pair_ids(ids)
    scores(0, z[pl.ds(0, R)], own_ids)
    scores(R, z[pl.ds(R, R)], own_ids)
    for piece in opening:
        pass_on(*piece)
    for axis in range(2):
        send_ids(axis).wait_recv()
        forward_ids(axis).start()
    send_ids(4).wait_recv()
    core_ids = pair_ids(r_ids.at[4])
    pass_on(1)
    to_core(0).wait_recv()
    scores(2 * R, core_z[pl.ds(0, R)], core_ids)
    pass_on(2)
    to_core(1).wait_recv()
    scores(3 * R, core_z[pl.ds(R, R)], core_ids)
    pass_on(3)
    for axis in range(2):
        forward_ids(axis).wait_recv()

    left = lax.broadcasted_iota(jnp.int32, (8, 128), 1) < 64

    def mixed(refs):
        a, b, c, d = (refs[p] for p in range(4))
        turn = lambda x: pltpu.roll(x, 64, 1)
        first = jnp.concatenate([jnp.where(left, a, turn(b)), jnp.where(left, c, turn(d))], axis=1)
        second = jnp.concatenate([jnp.where(left, turn(a), b), jnp.where(left, turn(c), d)], axis=1)
        return first, second

    first, second = mixed(r_ids)
    for q in range(2):
        id_rows[pl.ds(2 * q, 1)] = first[q : q + 1]
        id_rows[pl.ds(2 * q + 1, 1)] = second[q : q + 1]

    def stream_scores(c, pieces=None):
        for piece in pieces or [(c,)]:
            for axis in range(2):
                forward(axis, *piece).wait_recv()
        lane = pl.multiple_of(4 * R + 4 * CR * c, 4 * CR)
        scores(lane, streams[c].reshape(4 * CR, D), id_rows[pl.ds(c % 4, 1)])

    def stream_step(c, carry):
        stream_scores(c)
        pass_on(c + 4)
        return carry

    stream_scores(0, opening)
    pass_on(4)
    lax.fori_loop(1, CHUNKS - 5, stream_step, 0)
    stream_scores(CHUNKS - 5)
    pass_on(*last[0])
    pass_on(*last[1])
    end = CHUNKS - 1
    end_lane = 4 * R + 4 * CR * end
    end_ids = id_rows[pl.ds(end % 4, 1)]
    scores(end_lane, streams[end, pl.ds(0, 2)].reshape(2 * CR, D), end_ids[:, :128])
    for c in range(CHUNKS - 4, end):
        stream_scores(c)

    s_hi = den_acc[...].astype(BF16)
    rest = den_acc[...] - s_hi.astype(F32)
    s_mid, s_lo = split(rest)
    ones = jnp.ones((8, 128), BF16)
    inv_row[...] = jnp.zeros_like(inv_row)
    sums = dot_t(ones, s_hi) + dot_t(ones, s_mid) + dot_t(ones, s_lo)
    end_keep = jnp.concatenate([jnp.broadcast_to(end_ids[:, 128:], (128, 128)).T] * 4, axis=1) != jnp.concatenate(
        [own_ids, own_ids], axis=1
    )

    for piece in last:
        for axis in range(2):
            forward(axis, *piece).wait_recv()
    khi, klo = split(streams[end, pl.ds(2, 2)].reshape(2 * CR, D))
    turned = dot_t(khi, zl_hi[...]) + dot_t(klo, zl_hi[...]) + dot_t(khi, zl_lo[...])
    turned = jnp.where(end_keep, jnp.exp2(turned), 0.0)
    own_inv = 1.0 / (sums[0:1] + jnp.sum(turned, axis=0, keepdims=True))
    for q in range(4):
        inv_row[pl.ds(q, 1)] = own_inv[:, 128 * q : 128 * (q + 1)]
    for p in (2, 3, 0, 1, 4):
        send_inv(p).start()

    scores(end_lane + 128, streams[end, pl.ds(2, 2)].reshape(2 * CR, D), end_ids[:, 128:])
    for group in range(STEPS // 4):
        gather(group)
    centre = jnp.mean(own_inv, axis=1, keepdims=True)
    inv_col = 1.0 / jnp.sum(den_acc[...], axis=1, keepdims=True)
    coef = diag[...] * (inv_col[:R] + inv_col[R:]) - 1.0 / TAU
    for h in range(2):
        rows, others = pl.ds(R * h, R), pl.ds(R * (1 - h), R)
        acc[rows] = (inv_col[R * h : R * (h + 1)] + centre) * acc[rows] + coef * z[others]

    def spread(slot, row, lane, values):
        inv_rows[0:1, pl.ds(256 * slot + lane, values.shape[1])] = values[row : row + 1] - centre

    send_inv(4).wait_recv()
    own, other = inv_row[...], r_inv[4]
    for q in range(4):
        spread(q // 2, q, 128 * (q % 2), own)
        spread(2 + q // 2, q, 128 * (q % 2), other)
    acc[...] += weighted(e_hi, k_hi, inv_rows, pl.ds(0, 2 * R), pl.ds(0, 4 * R))

    whole(r_inv.at[pl.ds(0, 4)], den_send, den_recv.at[0]).wait_recv()
    first, second = mixed(r_inv)
    for q in range(4):
        spread(4 + 2 * q, q, 0, first)
        spread(5 + 2 * q, q, 0, second)

    for axis in range(2):
        whole(z, direct_send.at[axis], core_recv.at[0]).wait_send()
        whole(z, fwd_send.at[axis], core_recv.at[0]).wait_send()
    whole(z, core_send, core_recv.at[0]).wait_send()
    whole(r_ids, ids_send, core_recv.at[0]).wait_send()
    whole(r_inv, den_send, core_recv.at[0]).wait_send()


def weighted(e_hi, k_hi, inv_rows, rows, keys):
    off = jnp.broadcast_to(inv_rows[0:1, keys], (16, keys.size)).astype(BF16)[None]
    e = e_hi[rows, keys].reshape(rows.size // 16, 16, keys.size)
    return dot((e * off).reshape(rows.size, keys.size), k_hi[keys])


def finish(z, acc, inv_r, k_hi, e_hi, inv_rows, out_one, out_two, result, out_sem):
    outs = []
    for h in range(2):
        rows = pl.ds(R * h, R)
        g = acc[rows] + weighted(e_hi, k_hi, inv_rows, rows, pl.ds(4 * R, (STEPS - 4) * 256))
        own = z[rows]
        result[rows] = (g - own * jnp.sum(own * g, axis=1, keepdims=True)) * inv_r[rows]
        copy = pltpu.make_async_copy(result.at[rows], (out_one, out_two)[h], out_sem.at[h])
        copy.start()
        outs.append(copy)
    for copy in outs:
        copy.wait()


def on_device(view_one, view_two, node_ids):
    dma = pltpu.SemaphoreType.DMA
    hbm = pl.BlockSpec(memory_space=pltpu.HBM)
    vmem = pl.BlockSpec(memory_space=pltpu.VMEM)
    middle = pl.pallas_call(
        kernel,
        out_shape=(
            pltpu.VMEM((2 * R, D), F32),
            pltpu.VMEM((2 * R, D), F32),
            pltpu.VMEM((2 * R, 1), F32),
            pltpu.VMEM((256 * STEPS, D), BF16),
            pltpu.VMEM((2 * R, 256 * STEPS), BF16),
            pltpu.VMEM((8, 256 * STEPS), F32),
        ),
        in_specs=[hbm] * 3,
        out_specs=(vmem,) * 6,
        scratch_shapes=[
            pltpu.VMEM((2 * R, D), F32),
            pltpu.VMEM((2 * R, D), BF16),
            pltpu.VMEM((2 * R, D), BF16),
            pltpu.VMEM((2 * R, D), F32),
            pltpu.VMEM((CHUNKS, 4, CR, D), F32),
            pltpu.VMEM((256 * STEPS, D), BF16),
            pltpu.VMEM((2 * R, 256 * STEPS), BF16),
            pltpu.VMEM((2 * R, 128), F32),
            pltpu.VMEM((R, 128), F32),
            pltpu.VMEM((2, 128), jnp.int32),
            pltpu.VMEM((8, 128), F32),
            pltpu.VMEM((5, 8, 128), F32),
            pltpu.VMEM((8, 256), F32),
            pltpu.VMEM((8, 128), F32),
            pltpu.VMEM((5, 8, 128), F32),
            pltpu.VMEM((R, 1), F32),
            dma((3,)),
            dma((2,)),
            dma((2, CHUNKS + 2)),
            dma((2,)),
            dma((2, CHUNKS + 2)),
            dma,
            dma((2,)),
            dma,
            dma((5,)),
            dma,
            dma((2,)),
        ],
        compiler_params=pltpu.CompilerParams(
            collective_id=0, has_side_effects=True, vmem_limit_bytes=32 * 1024 * 1024
        ),
    )(*(pltpu.with_memory_space_constraint(x, pltpu.HBM) for x in (view_one, view_two, node_ids.reshape(2, 128))))
    return pl.pallas_call(
        finish,
        out_shape=(jax.ShapeDtypeStruct((R, D), F32), jax.ShapeDtypeStruct((R, D), F32)),
        in_specs=[vmem] * 6,
        out_specs=(hbm, hbm),
        scratch_shapes=[pltpu.VMEM((2 * R, D), F32), dma((2,))],
        compiler_params=pltpu.CompilerParams(vmem_limit_bytes=8 * 1024 * 1024),
    )(*middle)


def solution(mesh):
    rows = P(("blk", "grp"), None)
    return jax.shard_map(
        on_device,
        mesh=mesh,
        in_specs=(rows, rows, P(("blk", "grp"))),
        out_specs=(rows, rows),
        check_vma=False,
    )
```
